512 devices in a mesh: var: 16 (over z), lat: 32 (over x, y, core).
Axes of the slice: x: 4, y: 4, z: 16, core: 2. Of those that a mesh axis runs over, the one named last changes fastest.
Arguments:
- fields: bfloat16 [32, 16, 16384], P('var', None, 'lat'), may hold values from -6 to 6
- owner_table: int32 [16], replicated, may hold values from 0 to 15, as said below
- band_tokens: int32 [32], replicated, may hold values from 1 to 512, 12288 in all
- patch_weight: bfloat16 [32, 16, 1024], P('var'), may hold values from -1.5 to 1.5
- var_embed: bfloat16 [16, 1024], replicated, may hold values from -6 to 6
- key_query: bfloat16 [1024, 16], replicated, may hold values from -0.1875 to 0.1875
- value_weight: bfloat16 [1024, 1024], replicated, may hold values from -0.1875 to 0.1875
- out_weight: bfloat16 [1024, 1024], replicated, may hold values from -0.1875 to 0.1875
- cotangent: bfloat16 [32, 512, 1024], P('lat', 'var'), may hold values from -0.5 to 0.5
Outputs:
- aggregated: bfloat16 [32, 512, 1024], P('lat', 'var')
- d_value_weight: float32 [1024, 1024], P('lat')
- d_patch_weight: float32 [32, 16, 1024], P('var')
The draws below stay inside these ranges and needn't reach their ends.
Inputs may be any that keep to these rules, and one draw needn't show every extreme that they name: `owner_table`: each index of var owns at most 2 variables, and one owns exactly 2. The valid tokens of a band are its first band_tokens of 512; some band is full.
All inputs are finite; a program needn't handle non-finite values.
Results may differ from the reference program's by a relative error of at most 0.03.
Values may be sent and summed in bfloat16 or wider, within the bound.
A program may use at most 64 MiB of HBM per device.

```python
import math
import jax
import jax.numpy as jnp
import numpy as np
from jax import lax

D = 1024
H = 16
HD = 64
PATCH = 16
V = 16
SLOTS = 2
SLOTS_ALL = 32
TOK_LAT = 512
TOKENS = 16384
N_VAR = 16
N_LAT = 32


def draw_owner_table(key, part):
    key = jax.random.fold_in(key, 11)
    first_key, second_key, third_key = jax.random.split(key, 3)
    slot_count = 2 * V // N_VAR
    slot_total = slot_count * N_VAR
    busiest = jax.random.randint(first_key, (), 0, N_VAR)
    ranking = jax.random.permutation(second_key, slot_total).astype(jnp.int32)
    slot_owner = jnp.arange(slot_total, dtype=jnp.int32) // slot_count
    priority = ranking + slot_total * (slot_owner == busiest).astype(jnp.int32)
    unused_values, chosen = lax.top_k(priority, V)
    shuffle = jax.random.permutation(third_key, V)
    return (chosen[shuffle] // slot_count).astype(jnp.int32)


def block_levels(stream_key, dims, shards, least, high):
    factor_of, own = 1.0, jax.random.fold_in(stream_key, 6)
    for dim, blocks in shards:
        draws = jnp.exp(jax.random.uniform(jax.random.fold_in(own, dim), (blocks,), jnp.float32, least / len(shards), high / len(shards)))
        factor_of = factor_of * jnp.repeat(draws, dims[dim] // blocks).reshape([-1 if axis == dim else 1 for axis in range(len(dims))])
    return factor_of


def split_up(count, total, reach, skew):
    portions = [(1 << 20) // math.isqrt(grade ** skew) + 1 for grade in range(2, count + 1)]
    rest, holding = total - reach - (count - 1), [1] * (count - 1)
    while rest > 0:
        movable = [i for i in range(count - 1) if holding[i] < reach]
        mass, remaining = sum([portions[i] for i in movable]), rest
        for i in movable:
            more = min(reach - holding[i], max(1, remaining * portions[i] // mass), rest)
            holding[i] = holding[i] + more
            rest = rest - more
    return np.array([reach] + holding)


def ragged_sizes(rng, count, total, reach, lean):
    if count == 2:
        one = jax.random.randint(rng, (), max(1, total - reach), min(reach, total - 1) + 1)
        return jnp.stack([one, total - one])
    tallies = jnp.asarray(split_up(count, total, reach, lean), jnp.int32)
    couples = (count - 1) // 2
    giver, sink = tallies[1:1 + 2 * couples:2], tallies[2:2 + 2 * couples:2]
    margin = jnp.minimum(giver - 1, reach - sink)
    moved = jax.random.randint(jax.random.fold_in(rng, 1), (couples,), 0, 1 << 20) % (margin + 1)
    tallies = tallies.at[1:1 + 2 * couples:2].set(giver - moved).at[2:2 + 2 * couples:2].set(sink + moved)
    return tallies[jax.random.permutation(jax.random.fold_in(rng, 2), count)]


def bell_draw(own_key, extent, spread, most, cuts=(), kind=jnp.bfloat16):
    values = spread * jax.random.normal(own_key, extent, jnp.float32)
    if cuts:
        values = values * block_levels(own_key, extent, cuts, -0.22, 0.18)
    return jnp.clip(values, -most, most).astype(kind)


def setup_inputs(seed: int = 0) -> dict:
    seeds = jax.random.split(jax.random.key(seed), 10)
    fields = bell_draw(seeds[0], (SLOTS_ALL, PATCH, TOKENS), 1.0, 6.0, ((0, 16), (2, 32)))
    owner_table = draw_owner_table(jax.random.fold_in(seeds[9], 71), 0)
    band_tokens = ragged_sizes(seeds[2], N_LAT, TOK_LAT * N_LAT * 3 // 4, TOK_LAT, 2).astype(jnp.int32)
    patch_weight = bell_draw(seeds[3], (SLOTS_ALL, PATCH, D), PATCH ** -0.5, 1.5, ((0, 16),))
    var_embed = bell_draw(seeds[4], (V, D), 1.0, 6.0)
    key_query = bell_draw(seeds[5], (D, H), D ** -0.5, 0.1875)
    value_weight = bell_draw(seeds[6], (D, D), D ** -0.5, 0.1875)
    out_weight = bell_draw(seeds[7], (D, D), D ** -0.5, 0.1875)
    cotangent = bell_draw(seeds[8], (N_LAT, TOK_LAT, D), ((V / TOKENS) ** 0.5), 0.5, ((0, 32), (1, 16)))
    return {"fields": fields, "owner_table": owner_table, "band_tokens": band_tokens, "patch_weight": patch_weight, "var_embed": var_embed, "key_query": key_query, "value_weight": value_weight, "out_weight": out_weight, "cotangent": cotangent}


def slot_table(owner_table, slot_count):
    var_ids = jnp.arange(owner_table.shape[0], dtype=jnp.int32)
    same_owner = owner_table[:, None] == owner_table[None, :]
    earlier_var = var_ids[None, :] < var_ids[:, None]
    var_rank = jnp.sum((same_owner & earlier_var).astype(jnp.int32), axis=1)
    return (owner_table * slot_count + var_rank).astype(jnp.int32)


def reference(fields, owner_table, band_tokens, patch_weight, var_embed, key_query, value_weight, out_weight, cotangent):
    var_slot = slot_table(owner_table, SLOTS)
    var_fields = fields[var_slot]
    var_patch = patch_weight[var_slot].astype(jnp.float32)
    band_fields = var_fields.reshape(V, PATCH, N_LAT, TOK_LAT).transpose(2, 0, 1, 3)
    embed_rows = var_embed.astype(jnp.float32)[:, None, :]
    key_rows = key_query.astype(jnp.float32)

    def one_band(running, inputs):
        value_grad, patch_grad = running
        fields_now, band_count, band_cotangent = inputs
        embedded = (jnp.einsum("vkt,vkd->vtd", fields_now.astype(jnp.float32), var_patch) + embed_rows).astype(jnp.bfloat16)
        flattened = embedded.reshape(V * TOK_LAT, D)
        scores = jnp.dot(flattened, key_query, preferred_element_type=jnp.float32).reshape(V, TOK_LAT, H)
        exponent = jnp.exp(scores)
        attention = exponent / jnp.sum(exponent, axis=0)
        values = jnp.dot(flattened, value_weight, preferred_element_type=jnp.float32).astype(jnp.bfloat16)
        values = values.reshape(V, TOK_LAT, H, HD).astype(jnp.float32)
        pooled = jnp.sum(attention[..., None] * values, axis=0).astype(jnp.bfloat16).reshape(TOK_LAT, D)
        valid_mask = (jnp.arange(TOK_LAT) < band_count).astype(jnp.float32)[:, None]
        band_output = (valid_mask * jnp.dot(pooled, out_weight, preferred_element_type=jnp.float32)).astype(jnp.bfloat16)
        masked = valid_mask.astype(jnp.bfloat16) * band_cotangent
        head_grads = jnp.dot(masked, out_weight.T, preferred_element_type=jnp.float32).astype(jnp.bfloat16)
        head_grads = head_grads.reshape(TOK_LAT, H, HD).astype(jnp.float32)
        dvalues = (attention[..., None] * head_grads[None]).astype(jnp.bfloat16).reshape(V * TOK_LAT, D)
        dweights = jnp.sum(head_grads[None] * values, axis=-1)
        dscores = attention * (dweights - jnp.sum(attention * dweights, axis=0))
        value_grad = value_grad + lax.dot_general(flattened, dvalues, (((0,), (0,)), ((), ())), preferred_element_type=jnp.float32)
        embed_grad = jnp.dot(dvalues, value_weight.T, preferred_element_type=jnp.float32)
        embed_grad = embed_grad + jnp.dot(dscores.reshape(V * TOK_LAT, H), key_rows.T, precision=lax.Precision.HIGHEST)
        embed_grad = embed_grad.astype(jnp.bfloat16).reshape(V, TOK_LAT, D)
        patch_grad = patch_grad + jnp.einsum("vkt,vtd->vkd", fields_now.astype(jnp.float32), embed_grad.astype(jnp.float32))
        return (value_grad, patch_grad), band_output

    start_grads = (jnp.zeros((D, D), jnp.float32), jnp.zeros((V, PATCH, D), jnp.float32))
    (value_grad, patch_grad), aggregated = lax.scan(one_band, start_grads, (band_fields, band_tokens, cotangent))
    d_patch_weight = jnp.zeros((SLOTS_ALL, PATCH, D), jnp.float32).at[var_slot].set(patch_grad)
    return (aggregated, value_grad, d_patch_weight)
```

```python
import functools

import jax
import jax.numpy as jnp
from jax import lax
from jax.experimental import pallas as pl
from jax.experimental.pallas import tpu as pltpu
from jax.sharding import PartitionSpec as P

MESH = pl.DeviceIdType.MESH
F32 = jnp.float32
BF16 = jnp.bfloat16

NZ = 16
NP = 16
V = 16
K = 16
T = 32
D = 1024
TILES = 9
VK = V * K
TOK = NP * T


def dot(a, b, ca=1, cb=0):
    return lax.dot_general(a, b, (((ca,), (cb,)), ((), ())), preferred_element_type=F32)


def pooling_kernel(
    owner_ref,
    band_ref,
    fields_hbm,
    pw_hbm,
    ve_hbm,
    kq_hbm,
    vw_hbm,
    ow_hbm,
    cot_hbm,
    agg_ref,
    dvw_ref,
    dpw_ref,
    fields_v,
    pwve,
    kq_v,
    vwg,
    vw_v,
    ow_v,
    cot_v,
    msg1,
    recv1,
    krow,
    recvk,
    hmsg,
    recvh,
    mm,
    tmsg,
    recvf,
    recvp,
    aa,
    pmsg,
    recvpool,
    gtile,
    recvr,
    red,
    gtot,
    msg5,
    recv5,
    srow,
    recvs,
    load_sem,
    send_sem,
    recv_sem,
):
    z = lax.axis_index("var")
    lat = lax.axis_index("lat")
    core = lax.rem(lat, 2)
    p = lat // 2

    def zpeer(d):
        return {"var": lax.rem(z + d, NZ), "lat": lat}

    def plane_peer(chip):
        return {"var": z, "lat": chip * 2 + core}

    barrier = pltpu.get_barrier_semaphore()

    def signal_z(d, carry):
        pl.semaphore_signal(barrier, inc=1, device_id=zpeer(d), device_id_type=MESH)
        other = {"var": lax.rem(z + d, NZ), "lat": p * 2 + 1 - core}
        pl.semaphore_signal(barrier, inc=1, device_id=other, device_id_type=MESH)
        chip = lax.rem(p + d, NP)
        pl.semaphore_signal(barrier, inc=1, device_id=plane_peer(chip), device_id_type=MESH)
        return carry

    lax.fori_loop(1, NZ, signal_z, 0)
    pl.semaphore_signal(
        barrier, inc=1, device_id={"var": z, "lat": p * 2 + 1 - core}, device_id_type=MESH
    )

    group = pl.multiple_of((p // 2) * 128, 128)
    loads = [
        pltpu.make_async_copy(pw_hbm, pwve.at[pl.ds(0, 32)], load_sem.at[0]),
        pltpu.make_async_copy(ve_hbm, pwve.at[pl.ds(32, 16)], load_sem.at[1]),
        pltpu.make_async_copy(vw_hbm.at[:, pl.ds(group, 128)], vwg, load_sem.at[2]),
        pltpu.make_async_copy(kq_hbm, kq_v, load_sem.at[3]),
        pltpu.make_async_copy(fields_hbm, fields_v, load_sem.at[4]),
        pltpu.make_async_copy(cot_hbm, cot_v, load_sem.at[5]),
        pltpu.make_async_copy(ow_hbm, ow_v, load_sem.at[6]),
        pltpu.make_async_copy(vw_hbm, vw_v, load_sem.at[7]),
    ]
    for load in loads:
        load.start()

    owners = [owner_ref[v] for v in range(V)]
    slots = []
    for v in range(V):
        rank = jnp.int32(0)
        for u in range(v):
            rank = rank + (owners[u] == owners[v]).astype(jnp.int32)
        slots.append(owners[v] * 2 + rank)
    held = []
    for s in range(2):
        var_of, has = jnp.int32(0), jnp.int32(0)
        for v in range(V):
            hit = (slots[v] == 2 * z + s).astype(jnp.int32)
            var_of, has = var_of + hit * v, has + hit
        held.append((var_of, has))

    lane16 = lax.broadcasted_iota(jnp.int32, (16, 128), 1)
    row16 = lax.broadcasted_iota(jnp.int32, (16, 128), 0)
    lane32 = lax.broadcasted_iota(jnp.int32, (32, 128), 1)
    row32 = lax.broadcasted_iota(jnp.int32, (32, 128), 0)

    for i in range(5):
        loads[i].wait()
    turn = lax.rem(p, 2) * 64
    both = pwve[...]
    head_cols = pltpu.roll(dot(both, vwg[...]), turn, 1)
    key_cols = dot(both, kq_v[...])
    key_lane = lax.broadcasted_iota(jnp.int32, (48, 16), 1)
    key_col = jnp.sum(jnp.where(key_lane == p, key_cols, 0.0), axis=1, keepdims=True)
    key_bias = key_col[32:48]
    krow[...] = jnp.sum(
        jnp.where(lane32 == row32, key_col[0:32], 0.0), axis=0, keepdims=True
    )
    mm[V] = jnp.where(lane16 < 64, head_cols[32:48], 0.0).astype(BF16)
    slot_cols = head_cols[0:32]
    own_group = pl.multiple_of((lat // 4) * 128, 128)
    own_cols = pltpu.roll(
        pwve[pl.ds(0, 32), pl.ds(own_group, 128)].astype(F32),
        lax.rem(224 - 32 * lax.rem(lat, 4), 128),
        1,
    )
    base = jnp.where(lane32 < 64, slot_cols, own_cols)
    for q in range(4):
        tokens = fields_v[:, :, 128 * q : 128 * q + 128].reshape(32, 128).astype(F32)
        for r in range(4):
            turned = pltpu.roll(tokens, (64 - 32 * r) % 128, 1) if r != 2 else tokens
            piece = jnp.where((lane32 >= 64) & (lane32 < 96), turned, base)
            msg1[4 * q + r] = piece.astype(BF16).reshape(2, 16, 128)

    pl.semaphore_wait(barrier, 46)

    def copy1(d):
        return pltpu.make_async_remote_copy(
            src_ref=msg1.at[lax.rem(z + d, NZ)],
            dst_ref=recv1.at[pl.ds(2 * z, 2)],
            send_sem=send_sem.at[0],
            recv_sem=recv_sem.at[0],
            device_id=zpeer(d),
            device_id_type=MESH,
        )

    def copyk(d):
        return pltpu.make_async_remote_copy(
            src_ref=krow,
            dst_ref=recvk.at[z],
            send_sem=send_sem.at[1],
            recv_sem=recv_sem.at[1],
            device_id=zpeer(d),
            device_id_type=MESH,
        )

    def send1(d, carry):
        copy1(d).start()
        copyk(d).start()
        return carry

    lax.fori_loop(1, NZ, send1, 0)
    recv1[pl.ds(2 * z, 2)] = msg1[z]
    recvk[z] = krow[...]

    loads[5].wait()
    count = band_ref[lat]
    rows = z * T + lax.broadcasted_iota(jnp.int32, (T, 1), 0)
    valid = (rows < count).astype(F32)
    masked = (cot_v[...].astype(F32) * valid).astype(BF16)
    loads[6].wait()
    head_grads = dot(masked, ow_v[...], 1, 1)
    for q in range(8):
        two = head_grads[:, 128 * q : 128 * q + 128]
        hmsg[2 * q] = jnp.where(lane32 < 64, two, 0.0).astype(BF16)
        hmsg[2 * q + 1] = jnp.where(lane32 < 64, pltpu.roll(two, 64, 1), 0.0).astype(BF16)

    def plane_copy(src, dst, slot):
        def make(d):
            chip = lax.rem(p + d, NP)
            return pltpu.make_async_remote_copy(
                src_ref=src(chip),
                dst_ref=dst,
                send_sem=send_sem.at[slot],
                recv_sem=recv_sem.at[slot],
                device_id=plane_peer(chip),
                device_id_type=MESH,
            )

        return make

    def send_all(make):
        def body(d, carry):
            make(d).start()
            return carry

        lax.fori_loop(1, NP, body, 0)

    def whole(ref, slot):
        return pltpu.make_async_remote_copy(
            src_ref=ref,
            dst_ref=ref,
            send_sem=send_sem.at[slot],
            recv_sem=recv_sem.at[slot],
            device_id=zpeer(1),
            device_id_type=MESH,
        )

    send_all(plane_copy(lambda chip: hmsg.at[chip], recvh.at[p], 2))
    recvh[p] = hmsg[p]

    whole(recv1.at[pl.ds(0, 30)], 0).wait_recv()
    whole(recvk.at[pl.ds(0, 15)], 1).wait_recv()
    key_parts = []
    for v in range(V):
        mm[v] = recv1[slots[v]]
        row = recvk[slots[v] // 2]
        first = 16 * lax.rem(slots[v], 2)
        key_parts.append(
            jnp.sum(jnp.where(lane16 == row16 + first, row, 0.0), axis=1, keepdims=True)
        )
    key_rows = jnp.stack(key_parts)
    turned = mm[pl.ds(0, V)].reshape(VK, 128).astype(F32).T
    tmsg[...] = turned[64:128].astype(BF16).reshape(2, 32, VK)
    send_all(plane_copy(lambda chip: tmsg.at[0], recvf.at[p], 3))
    send_all(plane_copy(lambda chip: tmsg.at[1], recvp.at[p], 4))
    recvf[p] = tmsg[0]
    recvp[p] = tmsg[1]

    whole(recvf.at[pl.ds(0, 15)], 3).wait_recv()
    pixels = recvf[...].reshape(TOK, VK).astype(F32).T.reshape(V, K, TOK)
    scores = jnp.sum(pixels * key_rows, axis=1) + key_bias
    exponent = jnp.exp(scores)
    attention = exponent / jnp.sum(exponent, axis=0, keepdims=True)
    weighted = pixels * attention[:, None, :]
    aa[pl.ds(0, VK)] = weighted.reshape(VK, TOK).astype(BF16)
    aa[pl.ds(VK, V)] = attention.astype(BF16)
    whole(recvh.at[pl.ds(0, 15)], 2).wait_recv()
    grads = recvh[...].reshape(TOK, 128)
    head_weights = mm[...].reshape(VK + V, 128)
    lhs = aa[...]
    sums = dot(lhs, grads)
    cross = dot(head_weights, grads, 1, 1)
    dweights = jnp.sum(pixels * cross[0:VK].reshape(V, K, TOK), axis=1) + cross[VK : VK + V]
    dscores = attention * (
        dweights - jnp.sum(attention * dweights, axis=0, keepdims=True)
    )
    score_sums = jnp.sum(pixels * dscores[:, None, :], axis=2, keepdims=True)
    score_rows = jnp.sum(jnp.where(lane16 == 64 + row16, score_sums, 0.0), axis=1)
    dense = sums[0:128] + pltpu.roll(sums[128:256], 64, 1)
    gtile[pl.ds(0, 8)] = dense.astype(BF16).reshape(8, 16, 128)
    gtile[8] = (sums[VK : VK + V] + score_rows).astype(BF16)

    own_slot = 2 * z + core
    even = (lax.rem(z, 2) == 0) & (core == lax.rem(z // 2, 2))
    last = (z == 7) & (core == 0)
    own_tile = jnp.where(even, z // 2, TILES - 1)
    owns = even | last

    def send_tile(i, carry):
        to_z = jnp.where(i == TILES - 1, 7, 2 * i)
        to_core = jnp.where(i == TILES - 1, 0, lax.rem(i, 2))
        here = (to_z == z) & (to_core == core)

        @pl.when(jnp.logical_not(here))
        def _():
            pltpu.make_async_remote_copy(
                src_ref=gtile.at[i],
                dst_ref=recvr.at[own_slot],
                send_sem=send_sem.at[5],
                recv_sem=recv_sem.at[5],
                device_id={"var": to_z, "lat": p * 2 + to_core},
                device_id_type=MESH,
            ).start()

        return carry

    lax.fori_loop(0, TILES, send_tile, 0)

    def copy_total(d):
        there = lax.rem(own_slot + d, 2 * NZ)
        return pltpu.make_async_remote_copy(
            src_ref=red,
            dst_ref=gtot.at[own_tile],
            send_sem=send_sem.at[6],
            recv_sem=recv_sem.at[6],
            device_id={"var": there // 2, "lat": p * 2 + lax.rem(there, 2)},
            device_id_type=MESH,
        )

    @pl.when(owns)
    def _():
        recvr[own_slot] = gtile[own_tile]
        whole(recvr.at[pl.ds(0, 31)], 5).wait_recv()
        total = jnp.sum(recvr[...].astype(F32), axis=0).astype(BF16)
        red[...] = total
        gtot[own_tile] = total

        def body(d, carry):
            copy_total(d).start()
            return carry

        lax.fori_loop(1, 2 * NZ, body, 0)

    pooled = dot(lhs, head_weights, 0, 0)
    pmsg[...] = pooled.astype(BF16).reshape(NP, T, 128)
    send_all(plane_copy(lambda chip: pmsg.at[chip], recvpool.at[p], 7))
    recvpool[p] = pmsg[p]
    bias_rows = pwve[pl.ds(32, 16)]
    whole(recvpool.at[pl.ds(0, 15)], 7).wait_recv()
    parts = []
    for q in range(8):
        left = recvpool[2 * q].astype(F32)
        right = recvpool[2 * q + 1].astype(F32)
        parts.append(jnp.where(lane32 < 64, left, pltpu.roll(right, 64, 1)).astype(BF16))
    projected = dot(jnp.concatenate(parts, axis=1), ow_v[...])
    agg_ref[...] = (projected * valid).astype(BF16)

    whole(recvp.at[pl.ds(0, 15)], 4).wait_recv()

    @pl.when(owns)
    def _():
        whole(gtot.at[pl.ds(0, TILES - 1)], 6).wait_recv()

    @pl.when(jnp.logical_not(owns))
    def _():
        whole(gtot, 6).wait_recv()

    rows_all = recvp[...].reshape(TOK, VK)
    patch_sums = gtot[pl.ds(0, 8)].reshape(128, 128)
    bias_sums = gtot[8]
    low = dot(rows_all[:, 0:128], patch_sums)
    high = dot(rows_all[:, 128:256], patch_sums)
    bias_all = dot(bias_rows, bias_sums, 0, 0).reshape(NP, 2, T, 128)
    bias = jnp.where(core == 0, bias_all[:, 0], bias_all[:, 1])
    value_rows = (low + pltpu.roll(high, 64, 1)).reshape(NP, T, 128) + bias
    picked, score_parts = [], []
    for s in range(2):
        var_of, has = held[s]
        tile = gtot[lax.rem(var_of, 8)].astype(F32)
        tile = jnp.where(var_of < 8, pltpu.roll(tile, 64, 1), tile)
        picked.append(tile * has.astype(F32))
        line = jnp.where((row16 == var_of) & (lane16 >= 64) & (lane16 < 80), bias_sums.astype(F32), 0.0)
        line = jnp.sum(line, axis=0, keepdims=True) * has.astype(F32)
        score_parts.append(pltpu.roll(line, 64 + 16 * s, 1))
    mine = jnp.concatenate(picked, axis=0)
    srow[...] = score_parts[0] + score_parts[1]
    msg5[...] = jnp.where(lane32 < 64, value_rows, mine).astype(BF16)
    send_all(plane_copy(lambda chip: msg5.at[chip], recv5.at[p], 8))
    send_all(plane_copy(lambda chip: srow, recvs.at[p], 9))
    recv5[p] = msg5[p]
    recvs[p] = srow[...]

    loads[7].wait()
    whole(recv5.at[pl.ds(0, 15)], 8).wait_recv()
    whole(recvs.at[pl.ds(0, 15)], 9).wait_recv()
    parts = []
    for q in range(8):
        left = recv5[2 * q].astype(F32)
        right = recv5[2 * q + 1].astype(F32)
        dvw_ref[:, 128 * q : 128 * q + 128] = jnp.where(
            lane32 < 64, left, pltpu.roll(right, 64, 1)
        )
        parts.append(jnp.where(lane32 < 64, pltpu.roll(left, 64, 1), right).astype(BF16))
    patch_grad = dot(jnp.concatenate(parts, axis=1), vw_v[...], 1, 1)
    score_grad = recvs[...].reshape(NP, 128).T[0:32].astype(BF16)
    dpw_ref[...] = patch_grad + dot(score_grad, kq_v[...], 1, 1)

    whole(recv1.at[pl.ds(0, 30)], 0).wait_send()
    whole(recvk.at[pl.ds(0, 15)], 1).wait_send()
    whole(recvh.at[pl.ds(0, 15)], 2).wait_send()
    whole(recvf.at[pl.ds(0, 15)], 3).wait_send()
    whole(recvp.at[pl.ds(0, 15)], 4).wait_send()
    whole(recvpool.at[pl.ds(0, 15)], 7).wait_send()
    whole(recv5.at[pl.ds(0, 15)], 8).wait_send()
    whole(recvs.at[pl.ds(0, 15)], 9).wait_send()

    @pl.when(owns)
    def _():
        whole(gtot.at[pl.ds(0, TILES - 1)], 5).wait_send()
        whole(recvr.at[pl.ds(0, 31)], 6).wait_send()

    @pl.when(jnp.logical_not(owns))
    def _():
        whole(gtot, 5).wait_send()


def per_device(
    fields,
    owner_table,
    band_tokens,
    patch_weight,
    var_embed,
    key_query,
    value_weight,
    out_weight,
    cotangent,
):
    any_spec = pl.BlockSpec(memory_space=pl.ANY)
    smem_spec = pl.BlockSpec(memory_space=pltpu.SMEM)
    vmem_spec = pl.BlockSpec(memory_space=pltpu.VMEM)
    aggregated, value_grad, patch_grad = pl.pallas_call(
        pooling_kernel,
        out_shape=(
            jax.ShapeDtypeStruct((T, D), BF16),
            jax.ShapeDtypeStruct((32, D), F32),
            jax.ShapeDtypeStruct((32, D), F32),
        ),
        in_specs=[smem_spec] * 2 + [any_spec] * 7,
        out_specs=(vmem_spec, vmem_spec, vmem_spec),
        scratch_shapes=[
            pltpu.VMEM((2, K, 512), BF16),
            pltpu.VMEM((48, D), BF16),
            pltpu.VMEM((D, 16), BF16),
            pltpu.VMEM((D, 128), BF16),
            pltpu.VMEM((D, D), BF16),
            pltpu.VMEM((D, D), BF16),
            pltpu.VMEM((T, D), BF16),
            pltpu.VMEM((NZ, 2, K, 128), BF16),
            pltpu.VMEM((2 * NZ, K, 128), BF16),
            pltpu.VMEM((1, 128), F32),
            pltpu.VMEM((NZ, 1, 128), F32),
            pltpu.VMEM((NP, T, 128), BF16),
            pltpu.VMEM((NP, T, 128), BF16),
            pltpu.VMEM((V + 1, K, 128), BF16),
            pltpu.VMEM((2, T, VK), BF16),
            pltpu.VMEM((NP, T, VK), BF16),
            pltpu.VMEM((NP, T, VK), BF16),
            pltpu.VMEM((VK + V, TOK), BF16),
            pltpu.VMEM((NP, T, 128), BF16),
            pltpu.VMEM((NP, T, 128), BF16),
            pltpu.VMEM((TILES, 16, 128), BF16),
            pltpu.VMEM((2 * NZ, 16, 128), BF16),
            pltpu.VMEM((16, 128), BF16),
            pltpu.VMEM((TILES, 16, 128), BF16),
            pltpu.VMEM((NP, T, 128), BF16),
            pltpu.VMEM((NP, T, 128), BF16),
            pltpu.VMEM((1, 128), F32),
            pltpu.VMEM((NP, 1, 128), F32),
            pltpu.SemaphoreType.DMA((8,)),
            pltpu.SemaphoreType.DMA((10,)),
            pltpu.SemaphoreType.DMA((10,)),
        ],
        compiler_params=pltpu.CompilerParams(
            collective_id=0, has_side_effects=True, vmem_limit_bytes=32 * 1024 * 1024
        ),
        cost_estimate=pl.CostEstimate(
            flops=2_000_000_000, bytes_accessed=5_000_000, transcendentals=8192
        ),
    )(
        owner_table,
        band_tokens,
        fields,
        patch_weight.reshape(32, D),
        var_embed,
        key_query,
        value_weight,
        out_weight,
        cotangent.reshape(T, D),
    )
    return (
        aggregated.reshape(1, T, D),
        value_grad,
        patch_grad.reshape(2, K, D),
    )


def solution(mesh):
    in_specs = (
        P("var", None, "lat"),
        P(),
        P(),
        P("var", None, None),
        P(),
        P(),
        P(),
        P(),
        P("lat", "var", None),
    )
    out_specs = (P("lat", "var", None), P("lat", None), P("var", None, None))
    return jax.shard_map(
        per_device, mesh=mesh, in_specs=in_specs, out_specs=out_specs, check_vma=False
    )
```

```python
import functools

import jax
import jax.numpy as jnp
from jax import lax
from jax.experimental import pallas as pl
from jax.experimental.pallas import tpu as pltpu
from jax.sharding import PartitionSpec as P

MESH = pl.DeviceIdType.MESH
F32 = jnp.float32
BF16 = jnp.bfloat16

NZ = 16
NP = 16
V = 16
K = 16
T = 32
D = 1024
TILES = 9
FAR_FIRST = (8, 7, 9, 6, 10, 5, 11, 4, 12, 3, 13, 2, 14, 1, 15)
PLANE_STEPS = sorted(
    [(dx, dy) for dx in range(4) for dy in range(4) if dx or dy],
    key=lambda step: -sum(min(d, 4 - d) for d in step),
)
VK = V * K
TOK = NP * T


def dot(a, b, ca=1, cb=0):
    return lax.dot_general(a, b, (((ca,), (cb,)), ((), ())), preferred_element_type=F32)


def pooling_kernel(
    owner_ref,
    band_ref,
    fields_hbm,
    pw_hbm,
    ve_hbm,
    kq_hbm,
    vw_hbm,
    ow_hbm,
    cot_hbm,
    agg_ref,
    dvw_ref,
    dpw_ref,
    fields_v,
    pwve,
    kq_v,
    vwg,
    vw_v,
    ow_v,
    cot_v,
    fmsg,
    recv0,
    wmsg,
    recv1,
    hmsg,
    recvh,
    mm,
    fturn,
    pturn,
    recvf,
    recvp,
    aa,
    pmsg,
    recvpool,
    gtile,
    recvr,
    recvb,
    quad,
    quadb,
    recvq,
    recvqb,
    gtot,
    msg5,
    recv5,
    srow,
    recvs,
    load_sem,
    send_sem,
    recv_sem,
):
    z = lax.axis_index("var")
    lat = lax.axis_index("lat")
    core = lax.rem(lat, 2)
    p = lat // 2

    x, y = p // 4, lax.rem(p, 4)
    sibling = {"var": z, "lat": p * 2 + 1 - core}

    def zpeer(d):
        return {"var": lax.rem(z + d, NZ), "lat": lat}

    def plane_chip(step):
        return lax.rem(x + step[0], 4) * 4 + lax.rem(y + step[1], 4)

    def plane_peer(chip):
        return {"var": z, "lat": chip * 2 + core}

    def quad_device(j):
        return {"var": (z // 4) * 4 + lax.rem(j, 4), "lat": p * 2 + j // 4}

    barrier = pltpu.get_barrier_semaphore()

    def signal(device):
        pl.semaphore_signal(barrier, inc=1, device_id=device, device_id_type=MESH)

    own_j = core * 4 + lax.rem(z, 4)
    for d in FAR_FIRST:
        signal(zpeer(d))
    for step in PLANE_STEPS:
        signal(plane_peer(plane_chip(step)))
    signal(sibling)
    for d in range(1, 4):
        other = (z // 4) * 4 + lax.rem(z + d, 4)
        signal({"var": other, "lat": p * 2 + 1 - core})

    def whole(ref, slot):
        return pltpu.make_async_remote_copy(
            src_ref=ref,
            dst_ref=ref,
            send_sem=send_sem.at[slot],
            recv_sem=recv_sem.at[slot],
            device_id=sibling,
            device_id_type=MESH,
        )

    def send(src, dst, slot, device):
        pltpu.make_async_remote_copy(
            src_ref=src,
            dst_ref=dst,
            send_sem=send_sem.at[slot],
            recv_sem=recv_sem.at[slot],
            device_id=device,
            device_id_type=MESH,
        ).start()

    def send_plane(src, dst, slot):
        for step in PLANE_STEPS:
            chip = plane_chip(step)
            send(src(chip), dst, slot, plane_peer(chip))

    group = pl.multiple_of((p // 2) * 128, 128)
    loads = [
        pltpu.make_async_copy(fields_hbm, fields_v, load_sem.at[4]),
        pltpu.make_async_copy(pw_hbm, pwve.at[pl.ds(0, 32)], load_sem.at[0]),
        pltpu.make_async_copy(ve_hbm, pwve.at[pl.ds(32, 16)], load_sem.at[1]),
        pltpu.make_async_copy(vw_hbm.at[:, pl.ds(group, 128)], vwg, load_sem.at[2]),
        pltpu.make_async_copy(kq_hbm, kq_v, load_sem.at[3]),
        pltpu.make_async_copy(cot_hbm, cot_v, load_sem.at[5]),
        pltpu.make_async_copy(ow_hbm, ow_v, load_sem.at[6]),
        pltpu.make_async_copy(vw_hbm, vw_v, load_sem.at[7]),
    ]
    for load in loads:
        load.start()

    owners = [owner_ref[v] for v in range(V)]
    slots = []
    for v in range(V):
        rank = jnp.int32(0)
        for u in range(v):
            rank = rank + (owners[u] == owners[v]).astype(jnp.int32)
        slots.append(owners[v] * 2 + rank)
    held = []
    for s in range(2):
        var_of, has = jnp.int32(0), jnp.int32(0)
        for v in range(V):
            hit = (slots[v] == 2 * z + s).astype(jnp.int32)
            var_of, has = var_of + hit * v, has + hit
        held.append((var_of, has))

    lane16 = lax.broadcasted_iota(jnp.int32, (16, 128), 1)
    row16 = lax.broadcasted_iota(jnp.int32, (16, 128), 0)
    lane32 = lax.broadcasted_iota(jnp.int32, (32, 128), 1)
    row32 = lax.broadcasted_iota(jnp.int32, (32, 128), 0)

    loads[0].wait()
    for q in range(4):
        low = fields_v[0, :, 128 * q : 128 * q + 128].astype(F32)
        high = fields_v[1, :, 128 * q : 128 * q + 128].astype(F32)
        for r in range(4):
            left = pltpu.roll(low, (128 - 32 * r) % 128, 1) if r else low
            right = pltpu.roll(high, (160 - 32 * r) % 128, 1) if r != 1 else high
            piece = jnp.where(lane16 < 32, left, jnp.where(lane16 < 64, right, 0.0))
            fmsg[4 * q + r] = piece.astype(BF16)

    for i in range(1, 5):
        loads[i].wait()
    turn = lax.rem(p, 2) * 64
    both = pwve[...]
    head_cols = pltpu.roll(dot(both, vwg[...]), turn, 1)
    key_cols = dot(both, kq_v[...], 1, 1)
    key_lane = lax.broadcasted_iota(jnp.int32, (48, 16), 1)
    key_col = jnp.sum(jnp.where(key_lane == p, key_cols, 0.0), axis=1, keepdims=True)
    key_bias = key_col[32:48]
    mm[V] = jnp.where(lane16 < 64, head_cols[32:48], 0.0).astype(BF16)
    own_group = pl.multiple_of((lat // 4) * 128, 128)
    own_cols = pltpu.roll(
        pwve[pl.ds(0, 32), pl.ds(own_group, 128)].astype(F32),
        lax.rem(192 - 32 * lax.rem(lat, 4), 128),
        1,
    )
    key_top = key_col[0:32].astype(BF16).astype(F32)
    key_mid = (key_col[0:32] - key_top).astype(BF16).astype(F32)
    key_low = key_col[0:32] - key_top - key_mid
    packed = jnp.where(lane32 < 64, head_cols[0:32], own_cols)
    packed = jnp.where(lane32 < 96, packed, jnp.where(lane32 == 96, key_top, 0.0))
    packed = jnp.where(lane32 == 97, key_mid, jnp.where(lane32 == 98, key_low, packed))
    wmsg[...] = packed.astype(BF16).reshape(2, 16, 128)

    pl.semaphore_wait(barrier, 34)

    for d in FAR_FIRST:
        send(fmsg.at[lax.rem(z + d, NZ)], recv0.at[z], 0, zpeer(d))
    for d in FAR_FIRST:
        send(wmsg, recv1.at[pl.ds(2 * z, 2)], 1, zpeer(d))
    recv0[z] = fmsg[z]
    recv1[pl.ds(2 * z, 2)] = wmsg[...]

    loads[5].wait()
    count = band_ref[lat]
    rows = z * T + lax.broadcasted_iota(jnp.int32, (T, 1), 0)
    valid = (rows < count).astype(F32)
    masked = (cot_v[...].astype(F32) * valid).astype(BF16)
    loads[6].wait()
    head_grads = dot(masked, ow_v[...], 1, 1)
    for q in range(8):
        two = head_grads[:, 128 * q : 128 * q + 128]
        hmsg[2 * q] = jnp.where(lane32 < 64, two, 0.0).astype(BF16)
        hmsg[2 * q + 1] = jnp.where(lane32 < 64, pltpu.roll(two, 64, 1), 0.0).astype(BF16)

    send_plane(lambda chip: hmsg.at[chip], recvh.at[p], 2)
    recvh[p] = hmsg[p]

    whole(recv0.at[pl.ds(0, 15)], 0).wait_recv()
    pieces = []
    for v in range(V):
        tile = recv0[slots[v] // 2].astype(F32)
        pieces.append(pltpu.roll(tile, lax.rem(128 - 32 * lax.rem(slots[v], 2), 128), 1))
    fturn[...] = jnp.concatenate(pieces, axis=0).T[0:32].astype(BF16)
    send_plane(lambda chip: fturn, recvf.at[p], 3)
    recvf[p] = fturn[...]

    whole(recv1.at[pl.ds(0, 30)], 1).wait_recv()
    for v in range(V):
        mm[v] = recv1[slots[v]]
    chosen = mm[pl.ds(0, V)].reshape(VK, 128).astype(F32)
    lane_all = lax.broadcasted_iota(jnp.int32, (VK, 128), 1)
    key_rows = jnp.sum(
        jnp.where((lane_all >= 96) & (lane_all < 99), chosen, 0.0), axis=1, keepdims=True
    ).reshape(V, K, 1)
    pturn[...] = chosen.T[64:96].astype(BF16)

    whole(recvf.at[pl.ds(0, 15)], 3).wait_recv()
    pixels = recvf[...].reshape(TOK, VK).astype(F32).T.reshape(V, K, TOK)
    scores = jnp.sum(pixels * key_rows, axis=1) + key_bias
    exponent = jnp.exp(scores)
    attention = exponent / jnp.sum(exponent, axis=0, keepdims=True)
    weighted = pixels * attention[:, None, :]
    aa[pl.ds(0, VK)] = weighted.reshape(VK, TOK).astype(BF16)
    aa[pl.ds(VK, V)] = attention.astype(BF16)
    whole(recvh.at[pl.ds(0, 15)], 2).wait_recv()
    grads = recvh[...].reshape(TOK, 128)
    head_weights = mm[...].reshape(VK + V, 128)
    lhs = aa[...]
    sums = dot(lhs, grads)
    cross = dot(head_weights, grads, 1, 1)
    dweights = jnp.sum(pixels * cross[0:VK].reshape(V, K, TOK), axis=1) + cross[VK : VK + V]
    dscores = attention * (
        dweights - jnp.sum(attention * dweights, axis=0, keepdims=True)
    )
    score_sums = jnp.sum(pixels * dscores[:, None, :], axis=2, keepdims=True)
    score_rows = jnp.sum(jnp.where(lane16 == 64 + row16, score_sums, 0.0), axis=1)
    dense = sums[0:128] + pltpu.roll(sums[128:256], 64, 1)
    gtile[pl.ds(0, 8)] = dense.astype(BF16).reshape(8, 16, 128)
    gtile[8] = (sums[VK : VK + V] + score_rows).astype(BF16)

    for d in range(1, 8):
        j = lax.rem(own_j + d, 8)
        send(gtile.at[j], recvr.at[own_j], 5, quad_device(j))
    recvr[own_j] = gtile[own_j]
    has_bias = own_j == 1

    @pl.when(has_bias)
    def _():
        recvb[own_j] = gtile[8]

    @pl.when(jnp.logical_not(has_bias))
    def _():
        send(gtile.at[8], recvb.at[own_j], 6, quad_device(jnp.int32(1)))

    pooled = dot(lhs, head_weights, 0, 0)
    pmsg[...] = pooled.astype(BF16).reshape(NP, T, 128)
    send_plane(lambda chip: pmsg.at[chip], recvpool.at[p], 7)
    recvpool[p] = pmsg[p]
    send_plane(lambda chip: pturn, recvp.at[p], 4)
    recvp[p] = pturn[...]

    whole(recvr.at[pl.ds(0, 7)], 5).wait_recv()
    quad[...] = jnp.sum(recvr[...].astype(F32), axis=0).astype(BF16)
    for d in FAR_FIRST:
        send(quad, recvq.at[z], 10, zpeer(d))
    recvq[z] = quad[...]

    @pl.when(has_bias)
    def _():
        whole(recvb.at[pl.ds(0, 7)], 6).wait_recv()
        quadb[...] = jnp.sum(recvb[...].astype(F32), axis=0).astype(BF16)
        for d in FAR_FIRST:
            send(quadb, recvqb.at[z // 4], 11, zpeer(d))
        recvqb[z // 4] = quadb[...]

    bias_rows = pwve[pl.ds(32, 16)]
    whole(recvpool.at[pl.ds(0, 15)], 7).wait_recv()
    parts = []
    for q in range(8):
        left = recvpool[2 * q].astype(F32)
        right = recvpool[2 * q + 1].astype(F32)
        parts.append(jnp.where(lane32 < 64, left, pltpu.roll(right, 64, 1)).astype(BF16))
    projected = dot(jnp.concatenate(parts, axis=1), ow_v[...])
    agg_ref[...] = (projected * valid).astype(BF16)

    whole(recvp.at[pl.ds(0, 15)], 4).wait_recv()
    whole(recvq.at[pl.ds(0, 15)], 10).wait_recv()
    half = jnp.sum(recvq[...].astype(F32).reshape(4, 4, 16, 128), axis=0).astype(BF16)
    half_at = pl.multiple_of(5 * core, 5)
    gtot[pl.ds(half_at, 4)] = half

    @pl.when(core == 1)
    def _():
        gtot[9] = jnp.zeros((16, 128), BF16)

    @pl.when((core == 0) & has_bias)
    def _():
        whole(recvqb.at[pl.ds(0, 3)], 11).wait_recv()

    @pl.when((core == 0) & jnp.logical_not(has_bias))
    def _():
        whole(recvqb, 11).wait_recv()

    @pl.when(core == 0)
    def _():
        gtot[4] = jnp.sum(recvqb[...].astype(F32), axis=0).astype(BF16)

    send(gtot.at[pl.ds(half_at, 5)], gtot.at[pl.ds(half_at, 5)], 12, sibling)
    whole(gtot.at[pl.ds(0, 5)], 12).wait_recv()

    rows_all = recvp[...].reshape(TOK, VK)
    patch_sums = jnp.concatenate([gtot[pl.ds(0, 4)], gtot[pl.ds(5, 4)]], axis=0).reshape(128, 128)
    bias_sums = gtot[4]
    low = dot(rows_all[:, 0:128], patch_sums)
    high = dot(rows_all[:, 128:256], patch_sums)
    bias_all = dot(bias_rows, bias_sums, 0, 0).reshape(NP, 2, T, 128)
    bias = jnp.where(core == 0, bias_all[:, 0], bias_all[:, 1])
    value_rows = (low + pltpu.roll(high, 64, 1)).reshape(NP, T, 128) + bias
    picked, score_parts = [], []
    for s in range(2):
        var_of, has = held[s]
        at = lax.rem(var_of, 8)
        tile = gtot[at + at // 4].astype(F32)
        tile = jnp.where(var_of < 8, pltpu.roll(tile, 64, 1), tile)
        picked.append(tile * has.astype(F32))
        line = jnp.where((row16 == var_of) & (lane16 >= 64) & (lane16 < 80), bias_sums.astype(F32), 0.0)
        line = jnp.sum(line, axis=0, keepdims=True) * has.astype(F32)
        score_parts.append(pltpu.roll(line, 64 + 16 * s, 1))
    mine = jnp.concatenate(picked, axis=0)
    srow[...] = score_parts[0] + score_parts[1]
    msg5[...] = jnp.where(lane32 < 64, value_rows, mine).astype(BF16)
    send_plane(lambda chip: msg5.at[chip], recv5.at[p], 8)
    send_plane(lambda chip: srow, recvs.at[p], 9)
    recv5[p] = msg5[p]
    recvs[p] = srow[...]

    loads[7].wait()
    whole(recv5.at[pl.ds(0, 15)], 8).wait_recv()
    whole(recvs.at[pl.ds(0, 15)], 9).wait_recv()
    parts = []
    for q in range(8):
        left = recv5[2 * q].astype(F32)
        right = recv5[2 * q + 1].astype(F32)
        dvw_ref[:, 128 * q : 128 * q + 128] = jnp.where(
            lane32 < 64, left, pltpu.roll(right, 64, 1)
        )
        parts.append(jnp.where(lane32 < 64, pltpu.roll(left, 64, 1), right).astype(BF16))
    patch_grad = dot(jnp.concatenate(parts, axis=1), vw_v[...], 1, 1)
    score_grad = recvs[...].reshape(NP, 128).T[0:32].astype(BF16)
    dpw_ref[...] = patch_grad + dot(score_grad, kq_v[...])

    whole(recv0.at[pl.ds(0, 15)], 0).wait_send()
    whole(recv1.at[pl.ds(0, 30)], 1).wait_send()
    whole(recvh.at[pl.ds(0, 15)], 2).wait_send()
    whole(recvf.at[pl.ds(0, 15)], 3).wait_send()
    whole(recvp.at[pl.ds(0, 15)], 4).wait_send()
    whole(recvr.at[pl.ds(0, 7)], 5).wait_send()
    whole(recvpool.at[pl.ds(0, 15)], 7).wait_send()
    whole(recv5.at[pl.ds(0, 15)], 8).wait_send()
    whole(recvs.at[pl.ds(0, 15)], 9).wait_send()
    whole(recvq.at[pl.ds(0, 15)], 10).wait_send()
    whole(gtot.at[pl.ds(0, 5)], 12).wait_send()

    @pl.when(has_bias)
    def _():
        whole(recvq.at[pl.ds(0, 15)], 11).wait_send()

    @pl.when(jnp.logical_not(has_bias))
    def _():
        whole(quadb, 6).wait_send()


def per_device(
    fields,
    owner_table,
    band_tokens,
    patch_weight,
    var_embed,
    key_query,
    value_weight,
    out_weight,
    cotangent,
):
    hbm_spec = pl.BlockSpec(memory_space=pltpu.HBM)
    smem_spec = pl.BlockSpec(memory_space=pltpu.SMEM)
    vmem_spec = pl.BlockSpec(memory_space=pltpu.VMEM)
    aggregated, value_grad, patch_grad = pl.pallas_call(
        pooling_kernel,
        out_shape=(
            jax.ShapeDtypeStruct((T, D), BF16),
            jax.ShapeDtypeStruct((32, D), F32),
            jax.ShapeDtypeStruct((32, D), F32),
        ),
        in_specs=[smem_spec] * 2 + [hbm_spec] * 7,
        out_specs=(vmem_spec, vmem_spec, vmem_spec),
        scratch_shapes=[
            pltpu.VMEM((2, K, 512), BF16),
            pltpu.VMEM((48, D), BF16),
            pltpu.VMEM((16, D), BF16),
            pltpu.VMEM((D, 128), BF16),
            pltpu.VMEM((D, D), BF16),
            pltpu.VMEM((D, D), BF16),
            pltpu.VMEM((T, D), BF16),
            pltpu.VMEM((NZ, K, 128), BF16),
            pltpu.VMEM((NZ, K, 128), BF16),
            pltpu.VMEM((2, K, 128), BF16),
            pltpu.VMEM((2 * NZ, K, 128), BF16),
            pltpu.VMEM((NP, T, 128), BF16),
            pltpu.VMEM((NP, T, 128), BF16),
            pltpu.VMEM((V + 1, K, 128), BF16),
            pltpu.VMEM((T, VK), BF16),
            pltpu.VMEM((32, VK), BF16),
            pltpu.VMEM((NP, T, VK), BF16),
            pltpu.VMEM((NP, T, VK), BF16),
            pltpu.VMEM((VK + V, TOK), BF16),
            pltpu.VMEM((NP, T, 128), BF16),
            pltpu.VMEM((NP, T, 128), BF16),
            pltpu.VMEM((TILES, 16, 128), BF16),
            pltpu.VMEM((8, 16, 128), BF16),
            pltpu.VMEM((8, 16, 128), BF16),
            pltpu.VMEM((16, 128), BF16),
            pltpu.VMEM((16, 128), BF16),
            pltpu.VMEM((NZ, 16, 128), BF16),
            pltpu.VMEM((4, 16, 128), BF16),
            pltpu.VMEM((10, 16, 128), BF16),
            pltpu.VMEM((NP, T, 128), BF16),
            pltpu.VMEM((NP, T, 128), BF16),
            pltpu.VMEM((1, 128), F32),
            pltpu.VMEM((NP, 1, 128), F32),
            pltpu.SemaphoreType.DMA((8,)),
            pltpu.SemaphoreType.DMA((14,)),
            pltpu.SemaphoreType.DMA((14,)),
        ],
        compiler_params=pltpu.CompilerParams(
            collective_id=0, has_side_effects=True, vmem_limit_bytes=60 * 1024 * 1024
        ),
        cost_estimate=pl.CostEstimate(
            flops=2_000_000_000, bytes_accessed=5_000_000, transcendentals=8192
        ),
    )(
        owner_table,
        band_tokens,
        fields,
        patch_weight.reshape(32, D),
        var_embed,
        key_query.T,
        value_weight,
        out_weight,
        cotangent.reshape(T, D),
    )
    return (
        aggregated.reshape(1, T, D),
        value_grad,
        patch_grad.reshape(2, K, D),
    )


def solution(mesh):
    in_specs = (
        P("var", None, "lat"),
        P(),
        P(),
        P("var", None, None),
        P(),
        P(),
        P(),
        P(),
        P("lat", "var", None),
    )
    out_specs = (P("lat", "var", None), P("lat", None), P("var", None, None))
    return jax.shard_map(
        per_device, mesh=mesh, in_specs=in_specs, out_specs=out_specs, check_vma=False
    )
```

```python
import functools

import jax
import jax.numpy as jnp
from jax import lax
from jax.experimental import pallas as pl
from jax.experimental.pallas import tpu as pltpu
from jax.sharding import PartitionSpec as P

MESH = pl.DeviceIdType.MESH
F32 = jnp.float32
BF16 = jnp.bfloat16

NZ = 16
NP = 16
V = 16
K = 16
T = 32
D = 1024
TILES = 9
FAR_FIRST = (8, 7, 9, 6, 10, 5, 11, 4, 12, 3, 13, 2, 14, 1, 15)
PLANE_STEPS = sorted(
    [(dx, dy) for dx in range(4) for dy in range(4) if dx or dy],
    key=lambda step: -sum(min(d, 4 - d) for d in step),
)
VK = V * K
TOK = NP * T


def dot(a, b, ca=1, cb=0):
    return lax.dot_general(a, b, (((ca,), (cb,)), ((), ())), preferred_element_type=F32)


def pooling_kernel(
    owner_hbm,
    band_hbm,
    fields_hbm,
    pw_hbm,
    ve_hbm,
    kq_hbm,
    vw_hbm,
    ow_hbm,
    cot_hbm,
    agg_ref,
    dvw_ref,
    dpw_ref,
    owner_ref,
    band_ref,
    fields_v,
    pwve,
    kq_v,
    vwg,
    vw_v,
    ow_v,
    cot_v,
    fmsg,
    recv0,
    wmsg,
    recv1,
    hmsg,
    recvh,
    mm,
    fturn,
    pturn,
    recvf,
    recvp,
    aa,
    pmsg,
    recvpool,
    gtile,
    recvr,
    recvb,
    quad,
    quadb,
    recvq,
    recvqb,
    gtot,
    msg5,
    recv5,
    load_sem,
    send_sem,
    recv_sem,
):
    z = lax.axis_index("var")
    lat = lax.axis_index("lat")
    core = lax.rem(lat, 2)
    p = lat // 2

    x, y = p // 4, lax.rem(p, 4)
    sibling = {"var": z, "lat": p * 2 + 1 - core}

    def zpeer(d):
        return {"var": lax.rem(z + d, NZ), "lat": lat}

    def plane_chip(step):
        return lax.rem(x + step[0], 4) * 4 + lax.rem(y + step[1], 4)

    def plane_peer(chip):
        return {"var": z, "lat": chip * 2 + core}

    def quad_device(j):
        return {"var": (z // 4) * 4 + lax.rem(j, 4), "lat": p * 2 + j // 4}

    barrier = pltpu.get_barrier_semaphore()

    def signal(device):
        pl.semaphore_signal(barrier, inc=1, device_id=device, device_id_type=MESH)

    own_j = core * 4 + lax.rem(z, 4)
    for d in FAR_FIRST:
        signal(zpeer(d))
    for step in PLANE_STEPS:
        signal(plane_peer(plane_chip(step)))
    signal(sibling)
    for d in range(1, 4):
        other = (z // 4) * 4 + lax.rem(z + d, 4)
        signal({"var": other, "lat": p * 2 + 1 - core})

    def whole(ref, slot):
        return pltpu.make_async_remote_copy(
            src_ref=ref,
            dst_ref=ref,
            send_sem=send_sem.at[slot],
            recv_sem=recv_sem.at[slot],
            device_id=sibling,
            device_id_type=MESH,
        )

    def send(src, dst, slot, device):
        pltpu.make_async_remote_copy(
            src_ref=src,
            dst_ref=dst,
            send_sem=send_sem.at[slot],
            recv_sem=recv_sem.at[slot],
            device_id=device,
            device_id_type=MESH,
        ).start()

    def send_plane(src, dst, slot):
        for step in PLANE_STEPS:
            chip = plane_chip(step)
            send(src(chip), dst, slot, plane_peer(chip))

    group = pl.multiple_of((p // 2) * 128, 128)
    loads = [
        pltpu.make_async_copy(fields_hbm, fields_v, load_sem.at[4]),
        pltpu.make_async_copy(pw_hbm, pwve.at[pl.ds(0, 32)], load_sem.at[0]),
        pltpu.make_async_copy(ve_hbm, pwve.at[pl.ds(32, 16)], load_sem.at[1]),
        pltpu.make_async_copy(vw_hbm.at[:, pl.ds(group, 128)], vwg, load_sem.at[2]),
        pltpu.make_async_copy(kq_hbm, kq_v, load_sem.at[3]),
        pltpu.make_async_copy(cot_hbm, cot_v, load_sem.at[5]),
        pltpu.make_async_copy(ow_hbm, ow_v, load_sem.at[6]),
        pltpu.make_async_copy(vw_hbm, vw_v, load_sem.at[7]),
        pltpu.make_async_copy(owner_hbm, owner_ref, load_sem.at[8]),
        pltpu.make_async_copy(band_hbm, band_ref, load_sem.at[9]),
    ]
    for load in loads[8:] + loads[:8]:
        load.start()

    lane16 = lax.broadcasted_iota(jnp.int32, (16, 128), 1)
    row16 = lax.broadcasted_iota(jnp.int32, (16, 128), 0)
    lane32 = lax.broadcasted_iota(jnp.int32, (32, 128), 1)
    loads[0].wait()
    for q in range(4):
        low = fields_v[0, :, 128 * q : 128 * q + 128].astype(F32)
        high = fields_v[1, :, 128 * q : 128 * q + 128].astype(F32)
        for r in range(4):
            left = pltpu.roll(low, (128 - 32 * r) % 128, 1) if r else low
            right = pltpu.roll(high, (160 - 32 * r) % 128, 1) if r != 1 else high
            piece = jnp.where(lane16 < 32, left, jnp.where(lane16 < 64, right, 0.0))
            fmsg[4 * q + r] = piece.astype(BF16)

    loads[8].wait()
    owners = [owner_ref[v] for v in range(V)]
    slots = []
    for v in range(V):
        rank = jnp.int32(0)
        for u in range(v):
            rank = rank + (owners[u] == owners[v]).astype(jnp.int32)
        slots.append(owners[v] * 2 + rank)
    held = []
    for s in range(2):
        var_of, has = jnp.int32(0), jnp.int32(0)
        for v in range(V):
            hit = (slots[v] == 2 * z + s).astype(jnp.int32)
            var_of, has = var_of + hit * v, has + hit
        held.append((var_of, has))

    for i in range(1, 5):
        loads[i].wait()
    turn = lax.rem(p, 2) * 64
    both = pwve[...]
    head_cols = pltpu.roll(dot(both, vwg[...]), turn, 1)
    key_cols = dot(both, kq_v[...], 1, 1)
    key_lane = lax.broadcasted_iota(jnp.int32, (48, 16), 1)
    key_col = jnp.sum(jnp.where(key_lane == p, key_cols, 0.0), axis=1, keepdims=True)
    key_bias = key_col[32:48]
    mm[V] = jnp.where(lane16 < 64, head_cols[32:48], 0.0).astype(BF16)
    own_group = pl.multiple_of((lat // 4) * 128, 128)
    own_cols = pltpu.roll(
        pwve[pl.ds(0, 32), pl.ds(own_group, 128)].astype(F32),
        lax.rem(192 - 32 * lax.rem(lat, 4), 128),
        1,
    )
    key_top = key_col[0:32].astype(BF16).astype(F32)
    key_mid = (key_col[0:32] - key_top).astype(BF16).astype(F32)
    key_low = key_col[0:32] - key_top - key_mid
    packed = jnp.where(lane32 < 64, head_cols[0:32], own_cols)
    packed = jnp.where(lane32 < 96, packed, jnp.where(lane32 == 96, key_top, 0.0))
    packed = jnp.where(lane32 == 97, key_mid, jnp.where(lane32 == 98, key_low, packed))
    wmsg[...] = packed.astype(BF16).reshape(2, 16, 128)

    pl.semaphore_wait(barrier, 34)

    for d in FAR_FIRST:
        send(fmsg.at[lax.rem(z + d, NZ)], recv0.at[z], 0, zpeer(d))
    for d in FAR_FIRST:
        send(wmsg, recv1.at[pl.ds(2 * z, 2)], 1, zpeer(d))
    recv0[z] = fmsg[z]
    recv1[pl.ds(2 * z, 2)] = wmsg[...]

    loads[5].wait()
    loads[9].wait()
    count = band_ref[lat]
    rows = z * T + lax.broadcasted_iota(jnp.int32, (T, 1), 0)
    valid = (rows < count).astype(F32)
    masked = (cot_v[...].astype(F32) * valid).astype(BF16)
    loads[6].wait()
    head_grads = dot(masked, ow_v[...], 1, 1)
    for q in range(8):
        two = head_grads[:, 128 * q : 128 * q + 128]
        hmsg[2 * q] = jnp.where(lane32 < 64, two, 0.0).astype(BF16)
        hmsg[2 * q + 1] = jnp.where(lane32 < 64, pltpu.roll(two, 64, 1), 0.0).astype(BF16)

    send_plane(lambda chip: hmsg.at[chip], recvh.at[p], 2)
    recvh[p] = hmsg[p]

    whole(recv0.at[pl.ds(0, 15)], 0).wait_recv()
    pieces = []
    for v in range(V):
        tile = recv0[slots[v] // 2].astype(F32)
        pieces.append(pltpu.roll(tile, lax.rem(128 - 32 * lax.rem(slots[v], 2), 128), 1))
    fturn[...] = jnp.concatenate(pieces, axis=0).T[0:32].astype(BF16)
    send_plane(lambda chip: fturn, recvf.at[p], 3)
    recvf[p] = fturn[...]

    whole(recv1.at[pl.ds(0, 30)], 1).wait_recv()
    for v in range(V):
        mm[v] = recv1[slots[v]]
    chosen = mm[pl.ds(0, V)].reshape(VK, 128).astype(F32)
    lane_all = lax.broadcasted_iota(jnp.int32, (VK, 128), 1)
    key_rows = jnp.sum(
        jnp.where((lane_all >= 96) & (lane_all < 99), chosen, 0.0), axis=1, keepdims=True
    ).reshape(V, K, 1)
    pturn[...] = chosen.T[64:96].astype(BF16)
    send_plane(lambda chip: pturn, recvp.at[p], 4)
    recvp[p] = pturn[...]

    whole(recvf.at[pl.ds(0, 15)], 3).wait_recv()
    pixels = recvf[...].reshape(TOK, VK).astype(F32).T.reshape(V, K, TOK)
    scores = jnp.sum(pixels * key_rows, axis=1) + key_bias
    exponent = jnp.exp(scores)
    attention = exponent / jnp.sum(exponent, axis=0, keepdims=True)
    weighted = pixels * attention[:, None, :]
    aa[pl.ds(0, VK)] = weighted.reshape(VK, TOK).astype(BF16)
    aa[pl.ds(VK, V)] = attention.astype(BF16)
    whole(recvh.at[pl.ds(0, 15)], 2).wait_recv()
    grads = recvh[...].reshape(TOK, 128)
    head_weights = mm[...].reshape(VK + V, 128)
    lhs = aa[...]
    sums = dot(lhs, grads)
    cross = dot(head_weights, grads, 1, 1)
    dweights = jnp.sum(pixels * cross[0:VK].reshape(V, K, TOK), axis=1) + cross[VK : VK + V]
    dscores = attention * (
        dweights - jnp.sum(attention * dweights, axis=0, keepdims=True)
    )
    score_sums = jnp.sum(pixels * dscores[:, None, :], axis=2, keepdims=True)
    score_rows = jnp.sum(jnp.where(lane16 == 64 + row16, score_sums, 0.0), axis=1)
    dense = sums[0:128] + pltpu.roll(sums[128:256], 64, 1)
    gtile[pl.ds(0, 8)] = dense.astype(BF16).reshape(8, 16, 128)
    gtile[8] = (sums[VK : VK + V] + score_rows).astype(BF16)

    for d in range(1, 8):
        j = lax.rem(own_j + d, 8)
        send(gtile.at[j], recvr.at[own_j], 5, quad_device(j))
    recvr[own_j] = gtile[own_j]
    has_bias = own_j == 1

    @pl.when(has_bias)
    def _():
        recvb[own_j] = gtile[8]

    @pl.when(jnp.logical_not(has_bias))
    def _():
        send(gtile.at[8], recvb.at[own_j], 6, quad_device(jnp.int32(1)))

    pooled = dot(lhs, head_weights, 0, 0)
    pmsg[...] = pooled.astype(BF16).reshape(NP, T, 128)

    whole(recvr.at[pl.ds(0, 7)], 5).wait_recv()
    quad[...] = jnp.sum(recvr[...].astype(F32), axis=0).astype(BF16)
    for d in FAR_FIRST:
        send(quad, recvq.at[z], 10, zpeer(d))
    recvq[z] = quad[...]

    @pl.when(has_bias)
    def _():
        whole(recvb.at[pl.ds(0, 7)], 6).wait_recv()
        quadb[...] = jnp.sum(recvb[...].astype(F32), axis=0).astype(BF16)
        for d in FAR_FIRST:
            send(quadb, recvqb.at[z // 4], 11, zpeer(d))
        recvqb[z // 4] = quadb[...]

    send_plane(lambda chip: pmsg.at[chip], recvpool.at[p], 7)
    recvpool[p] = pmsg[p]

    whole(recvp.at[pl.ds(0, 15)], 4).wait_recv()
    whole(recvq.at[pl.ds(0, 15)], 10).wait_recv()
    half = jnp.sum(recvq[...].astype(F32).reshape(4, 4, 16, 128), axis=0).astype(BF16)
    half_at = pl.multiple_of(5 * core, 5)
    gtot[pl.ds(half_at, 4)] = half

    @pl.when(core == 1)
    def _():
        gtot[9] = jnp.zeros((16, 128), BF16)

    @pl.when((core == 0) & has_bias)
    def _():
        whole(recvqb.at[pl.ds(0, 3)], 11).wait_recv()

    @pl.when((core == 0) & jnp.logical_not(has_bias))
    def _():
        whole(recvqb, 11).wait_recv()

    @pl.when(core == 0)
    def _():
        gtot[4] = jnp.sum(recvqb[...].astype(F32), axis=0).astype(BF16)

    send(gtot.at[pl.ds(half_at, 5)], gtot.at[pl.ds(half_at, 5)], 12, sibling)
    whole(gtot.at[pl.ds(0, 5)], 12).wait_recv()

    bias_rows = pwve[pl.ds(32, 16)]
    rows_all = recvp[...].reshape(TOK, VK)
    patch_sums = jnp.concatenate([gtot[pl.ds(0, 4)], gtot[pl.ds(5, 4)]], axis=0).reshape(128, 128)
    bias_sums = gtot[4]
    low = dot(rows_all[:, 0:128], patch_sums)
    high = dot(rows_all[:, 128:256], patch_sums)
    bias_all = dot(bias_rows, bias_sums, 0, 0).reshape(NP, 2, T, 128)
    bias = jnp.where(core == 0, bias_all[:, 0], bias_all[:, 1])
    value_rows = (low + pltpu.roll(high, 64, 1)).reshape(NP, T, 128) + bias
    picked, score_parts = [], []
    for s in range(2):
        var_of, has = held[s]
        at = lax.rem(var_of, 8)
        tile = gtot[at + at // 4].astype(F32)
        tile = jnp.where(var_of < 8, pltpu.roll(tile, 64, 1), tile)
        picked.append(tile * has.astype(F32))
        line = jnp.where((row16 == var_of) & (lane16 >= 64) & (lane16 < 80), bias_sums.astype(F32), 0.0)
        line = jnp.sum(line, axis=0, keepdims=True) * has.astype(F32)
        score_parts.append(pltpu.roll(line, 64 + 16 * s, 1))
    mine = jnp.concatenate(picked, axis=0)
    score_line = jnp.broadcast_to(score_parts[0] + score_parts[1], (16, 128)).astype(BF16)
    msg5[:, 0:32, :] = jnp.where(lane32 < 64, value_rows, mine).astype(BF16)
    msg5[:, 32:48, :] = jnp.broadcast_to(score_line, (NP, 16, 128))
    send_plane(lambda chip: msg5.at[chip], recv5.at[p], 8)
    recv5[p] = msg5[p]

    whole(recvpool.at[pl.ds(0, 15)], 7).wait_recv()
    parts = []
    for q in range(8):
        left = recvpool[2 * q].astype(F32)
        right = recvpool[2 * q + 1].astype(F32)
        parts.append(jnp.where(lane32 < 64, left, pltpu.roll(right, 64, 1)).astype(BF16))
    projected = dot(jnp.concatenate(parts, axis=1), ow_v[...])
    agg_ref[...] = (projected * valid).astype(BF16)

    loads[7].wait()
    whole(recv5.at[pl.ds(0, 15)], 8).wait_recv()
    parts = []
    for q in range(8):
        left = recv5[2 * q, 0:32].astype(F32)
        right = recv5[2 * q + 1, 0:32].astype(F32)
        dvw_ref[:, 128 * q : 128 * q + 128] = jnp.where(
            lane32 < 64, left, pltpu.roll(right, 64, 1)
        )
        parts.append(jnp.where(lane32 < 64, pltpu.roll(left, 64, 1), right).astype(BF16))
    patch_grad = dot(jnp.concatenate(parts, axis=1), vw_v[...], 1, 1)
    score_lines = jnp.zeros((16, 128), F32)
    for chip in range(NP):
        line = recv5[chip, 32:48].astype(F32)
        score_lines = jnp.where(row16 == chip, line, score_lines)
    score_grad = score_lines.T[0:32].astype(BF16)
    dpw_ref[...] = patch_grad + dot(score_grad, kq_v[...])

    whole(recv0.at[pl.ds(0, 15)], 0).wait_send()
    whole(recv1.at[pl.ds(0, 30)], 1).wait_send()
    whole(recvh.at[pl.ds(0, 15)], 2).wait_send()
    whole(recvf.at[pl.ds(0, 15)], 3).wait_send()
    whole(recvp.at[pl.ds(0, 15)], 4).wait_send()
    whole(recvr.at[pl.ds(0, 7)], 5).wait_send()
    whole(recvpool.at[pl.ds(0, 15)], 7).wait_send()
    whole(recv5.at[pl.ds(0, 15)], 8).wait_send()
    whole(recvq.at[pl.ds(0, 15)], 10).wait_send()
    whole(gtot.at[pl.ds(0, 5)], 12).wait_send()

    @pl.when(has_bias)
    def _():
        whole(recvq.at[pl.ds(0, 15)], 11).wait_send()

    @pl.when(jnp.logical_not(has_bias))
    def _():
        whole(quadb, 6).wait_send()


def place_kernel(*refs):
    sources, results, sems = refs[:3], refs[3:6], refs[6]
    stores = [pltpu.make_async_copy(sources[i], results[i], sems.at[i]) for i in range(3)]
    for store in stores:
        store.start()
    for store in stores:
        store.wait()


def per_device(
    fields,
    owner_table,
    band_tokens,
    patch_weight,
    var_embed,
    key_query,
    value_weight,
    out_weight,
    cotangent,
):
    hbm_spec = pl.BlockSpec(memory_space=pltpu.HBM)
    vmem_spec = pl.BlockSpec(memory_space=pltpu.VMEM)
    aggregated, value_grad, patch_grad = pl.pallas_call(
        pooling_kernel,
        out_shape=(
            pltpu.VMEM((T, D), BF16),
            pltpu.VMEM((32, D), F32),
            pltpu.VMEM((32, D), F32),
        ),
        in_specs=[hbm_spec] * 9,
        out_specs=(vmem_spec, vmem_spec, vmem_spec),
        scratch_shapes=[
            pltpu.SMEM((V,), jnp.int32),
            pltpu.SMEM((2 * NP,), jnp.int32),
            pltpu.VMEM((2, K, 512), BF16),
            pltpu.VMEM((48, D), BF16),
            pltpu.VMEM((16, D), BF16),
            pltpu.VMEM((D, 128), BF16),
            pltpu.VMEM((D, D), BF16),
            pltpu.VMEM((D, D), BF16),
            pltpu.VMEM((T, D), BF16),
            pltpu.VMEM((NZ, K, 128), BF16),
            pltpu.VMEM((NZ, K, 128), BF16),
            pltpu.VMEM((2, K, 128), BF16),
            pltpu.VMEM((2 * NZ, K, 128), BF16),
            pltpu.VMEM((NP, T, 128), BF16),
            pltpu.VMEM((NP, T, 128), BF16),
            pltpu.VMEM((V + 1, K, 128), BF16),
            pltpu.VMEM((T, VK), BF16),
            pltpu.VMEM((32, VK), BF16),
            pltpu.VMEM((NP, T, VK), BF16),
            pltpu.VMEM((NP, T, VK), BF16),
            pltpu.VMEM((VK + V, TOK), BF16),
            pltpu.VMEM((NP, T, 128), BF16),
            pltpu.VMEM((NP, T, 128), BF16),
            pltpu.VMEM((TILES, 16, 128), BF16),
            pltpu.VMEM((8, 16, 128), BF16),
            pltpu.VMEM((8, 16, 128), BF16),
            pltpu.VMEM((16, 128), BF16),
            pltpu.VMEM((16, 128), BF16),
            pltpu.VMEM((NZ, 16, 128), BF16),
            pltpu.VMEM((4, 16, 128), BF16),
            pltpu.VMEM((10, 16, 128), BF16),
            pltpu.VMEM((NP, 48, 128), BF16),
            pltpu.VMEM((NP, 48, 128), BF16),
            pltpu.SemaphoreType.DMA((10,)),
            pltpu.SemaphoreType.DMA((14,)),
            pltpu.SemaphoreType.DMA((14,)),
        ],
        compiler_params=pltpu.CompilerParams(
            collective_id=0, has_side_effects=True, vmem_limit_bytes=60 * 1024 * 1024
        ),
        cost_estimate=pl.CostEstimate(
            flops=2_000_000_000, bytes_accessed=5_000_000, transcendentals=8192
        ),
    )(
        owner_table,
        band_tokens,
        fields,
        patch_weight.reshape(32, D),
        var_embed,
        key_query.T,
        value_weight,
        out_weight,
        cotangent.reshape(T, D),
    )
    aggregated, value_grad, patch_grad = pl.pallas_call(
        place_kernel,
        out_shape=(
            jax.ShapeDtypeStruct((T, D), BF16),
            jax.ShapeDtypeStruct((32, D), F32),
            jax.ShapeDtypeStruct((32, D), F32),
        ),
        in_specs=[hbm_spec] * 3,
        out_specs=(hbm_spec,) * 3,
        scratch_shapes=[pltpu.SemaphoreType.DMA((3,))],
        compiler_params=pltpu.CompilerParams(vmem_limit_bytes=4 * 1024 * 1024),
    )(aggregated, value_grad, patch_grad)
    return (
        aggregated.reshape(1, T, D),
        value_grad,
        patch_grad.reshape(2, K, D),
    )


def solution(mesh):
    in_specs = (
        P("var", None, "lat"),
        P(),
        P(),
        P("var", None, None),
        P(),
        P(),
        P(),
        P(),
        P("lat", "var", None),
    )
    out_specs = (P("lat", "var", None), P("lat", None), P("var", None, None))
    return jax.shard_map(
        per_device, mesh=mesh, in_specs=in_specs, out_specs=out_specs, check_vma=False
    )
```

```python
import functools

import jax
import jax.numpy as jnp
from jax import lax
from jax.experimental import pallas as pl
from jax.experimental.pallas import tpu as pltpu
from jax.sharding import PartitionSpec as P

MESH = pl.DeviceIdType.MESH
F32 = jnp.float32
BF16 = jnp.bfloat16

NZ = 16
NP = 16
V = 16
K = 16
T = 32
D = 1024
TILES = 9
FAR_FIRST = (8, 7, 9, 6, 10, 5, 11, 4, 12, 3, 13, 2, 14, 1, 15)
PLANE_STEPS = sorted(
    [(dx, dy) for dx in range(4) for dy in range(4) if dx or dy],
    key=lambda step: -sum(min(d, 4 - d) for d in step),
)
VK = V * K
TOK = NP * T


def dot(a, b, ca=1, cb=0):
    return lax.dot_general(a, b, (((ca,), (cb,)), ((), ())), preferred_element_type=F32)


def pooling_kernel(
    owner_hbm,
    band_hbm,
    fields_hbm,
    pw_hbm,
    ve_hbm,
    kq_hbm,
    vw_hbm,
    ow_hbm,
    cot_hbm,
    agg_ref,
    dvw_ref,
    dpw_ref,
    owner_ref,
    band_ref,
    fields_v,
    pwve,
    kq_v,
    vwg,
    vw_v,
    ow_v,
    cot_v,
    fmsg,
    recv0,
    wmsg,
    recv1,
    hmsg,
    recvh,
    mm,
    fturn,
    pturn,
    recvf,
    recvp,
    aa,
    pmsg,
    recvpool,
    gtile,
    recvr,
    recvb,
    quad,
    quadb,
    recvq,
    recvqb,
    gtot,
    msg5,
    recv5,
    load_sem,
    send_sem,
    recv_sem,
):
    z = lax.axis_index("var")
    lat = lax.axis_index("lat")
    core = lax.rem(lat, 2)
    p = lat // 2

    x, y = p // 4, lax.rem(p, 4)
    sibling = {"var": z, "lat": p * 2 + 1 - core}

    def zpeer(d):
        return {"var": lax.rem(z + d, NZ), "lat": lat}

    def plane_chip(step):
        return lax.rem(x + step[0], 4) * 4 + lax.rem(y + step[1], 4)

    def plane_peer(chip):
        return {"var": z, "lat": chip * 2 + core}

    def quad_device(j):
        return {"var": (z // 4) * 4 + lax.rem(j, 4), "lat": p * 2 + j // 4}

    barrier = pltpu.get_barrier_semaphore()

    def signal(device):
        pl.semaphore_signal(barrier, inc=1, device_id=device, device_id_type=MESH)

    own_j = core * 4 + lax.rem(z, 4)
    for d in FAR_FIRST:
        signal(zpeer(d))
    for step in PLANE_STEPS:
        signal(plane_peer(plane_chip(step)))
    signal(sibling)
    for d in range(1, 4):
        other = (z // 4) * 4 + lax.rem(z + d, 4)
        signal({"var": other, "lat": p * 2 + 1 - core})

    def whole(ref, slot):
        return pltpu.make_async_remote_copy(
            src_ref=ref,
            dst_ref=ref,
            send_sem=send_sem.at[slot],
            recv_sem=recv_sem.at[slot],
            device_id=sibling,
            device_id_type=MESH,
        )

    def send(src, dst, slot, device):
        pltpu.make_async_remote_copy(
            src_ref=src,
            dst_ref=dst,
            send_sem=send_sem.at[slot],
            recv_sem=recv_sem.at[slot],
            device_id=device,
            device_id_type=MESH,
        ).start()

    def send_plane(src, dst, slot):
        for step in PLANE_STEPS:
            chip = plane_chip(step)
            send(src(chip), dst, slot, plane_peer(chip))

    group = pl.multiple_of((p // 2) * 128, 128)
    loads = [
        pltpu.make_async_copy(fields_hbm, fields_v, load_sem.at[4]),
        pltpu.make_async_copy(pw_hbm, pwve.at[pl.ds(0, 32)], load_sem.at[0]),
        pltpu.make_async_copy(ve_hbm, pwve.at[pl.ds(32, 16)], load_sem.at[1]),
        pltpu.make_async_copy(vw_hbm.at[:, pl.ds(group, 128)], vwg, load_sem.at[2]),
        pltpu.make_async_copy(kq_hbm, kq_v, load_sem.at[3]),
        pltpu.make_async_copy(cot_hbm, cot_v, load_sem.at[5]),
        pltpu.make_async_copy(ow_hbm, ow_v, load_sem.at[6]),
        pltpu.make_async_copy(vw_hbm, vw_v, load_sem.at[7]),
        pltpu.make_async_copy(owner_hbm, owner_ref, load_sem.at[8]),
        pltpu.make_async_copy(band_hbm, band_ref, load_sem.at[9]),
    ]
    for load in loads[8:] + loads[:8]:
        load.start()

    lane16 = lax.broadcasted_iota(jnp.int32, (16, 128), 1)
    row16 = lax.broadcasted_iota(jnp.int32, (16, 128), 0)
    lane32 = lax.broadcasted_iota(jnp.int32, (32, 128), 1)
    loads[0].wait()
    for q in range(4):
        low = fields_v[0, :, 128 * q : 128 * q + 128].astype(F32)
        high = fields_v[1, :, 128 * q : 128 * q + 128].astype(F32)
        for r in range(4):
            left = pltpu.roll(low, (128 - 32 * r) % 128, 1) if r else low
            right = pltpu.roll(high, (160 - 32 * r) % 128, 1) if r != 1 else high
            piece = jnp.where(lane16 < 32, left, jnp.where(lane16 < 64, right, 0.0))
            fmsg[4 * q + r] = piece.astype(BF16)

    loads[8].wait()
    owners = [owner_ref[v] for v in range(V)]
    slots = []
    for v in range(V):
        rank = jnp.int32(0)
        for u in range(v):
            rank = rank + (owners[u] == owners[v]).astype(jnp.int32)
        slots.append(owners[v] * 2 + rank)
    held = []
    for s in range(2):
        var_of, has = jnp.int32(0), jnp.int32(0)
        for v in range(V):
            hit = (slots[v] == 2 * z + s).astype(jnp.int32)
            var_of, has = var_of + hit * v, has + hit
        held.append((var_of, has))

    for i in range(1, 5):
        loads[i].wait()
    turn = lax.rem(p, 2) * 64
    both = pwve[...]
    head_cols = pltpu.roll(dot(both, vwg[...]), turn, 1)
    key_cols = dot(both, kq_v[...], 1, 1)
    key_lane = lax.broadcasted_iota(jnp.int32, (48, 16), 1)
    key_col = jnp.sum(jnp.where(key_lane == p, key_cols, 0.0), axis=1, keepdims=True)
    key_bias = key_col[32:48]
    mm[V] = jnp.where(lane16 < 64, head_cols[32:48], 0.0).astype(BF16)
    own_group = pl.multiple_of((lat // 4) * 128, 128)
    own_cols = pltpu.roll(
        pwve[pl.ds(0, 32), pl.ds(own_group, 128)].astype(F32),
        lax.rem(192 - 32 * lax.rem(lat, 4), 128),
        1,
    )
    key_top = key_col[0:32].astype(BF16).astype(F32)
    key_mid = (key_col[0:32] - key_top).astype(BF16).astype(F32)
    key_low = key_col[0:32] - key_top - key_mid
    packed = jnp.where(lane32 < 64, head_cols[0:32], own_cols)
    packed = jnp.where(lane32 < 96, packed, jnp.where(lane32 == 96, key_top, 0.0))
    packed = jnp.where(lane32 == 97, key_mid, jnp.where(lane32 == 98, key_low, packed))
    wmsg[...] = packed.astype(BF16).reshape(2, 16, 128)

    pl.semaphore_wait(barrier, 34)

    for d in FAR_FIRST:
        send(fmsg.at[lax.rem(z + d, NZ)], recv0.at[z], 0, zpeer(d))
    for d in FAR_FIRST:
        send(wmsg, recv1.at[pl.ds(2 * z, 2)], 1, zpeer(d))
    recv0[z] = fmsg[z]
    recv1[pl.ds(2 * z, 2)] = wmsg[...]

    loads[5].wait()
    loads[9].wait()
    count = band_ref[lat]
    rows = z * T + lax.broadcasted_iota(jnp.int32, (T, 1), 0)
    valid = (rows < count).astype(F32)
    masked = (cot_v[...].astype(F32) * valid).astype(BF16)
    loads[6].wait()
    head_grads = dot(masked, ow_v[...], 1, 1)
    for q in range(8):
        two = head_grads[:, 128 * q : 128 * q + 128]
        hmsg[2 * q] = jnp.where(lane32 < 64, two, 0.0).astype(BF16)
        hmsg[2 * q + 1] = jnp.where(lane32 < 64, pltpu.roll(two, 64, 1), 0.0).astype(BF16)

    send_plane(lambda chip: hmsg.at[chip], recvh.at[p], 2)
    recvh[p] = hmsg[p]

    whole(recv0.at[pl.ds(0, 15)], 0).wait_recv()
    pieces = []
    for v in range(V):
        tile = recv0[slots[v] // 2].astype(F32)
        pieces.append(pltpu.roll(tile, lax.rem(128 - 32 * lax.rem(slots[v], 2), 128), 1))
    fturn[...] = jnp.concatenate(pieces, axis=0).T[0:32].astype(BF16)
    send_plane(lambda chip: fturn, recvf.at[p], 3)
    recvf[p] = fturn[...]

    whole(recv1.at[pl.ds(0, 30)], 1).wait_recv()
    for v in range(V):
        mm[v] = recv1[slots[v]]
    chosen = mm[pl.ds(0, V)].reshape(VK, 128).astype(F32)
    lane_all = lax.broadcasted_iota(jnp.int32, (VK, 128), 1)
    key_rows = jnp.sum(
        jnp.where((lane_all >= 96) & (lane_all < 99), chosen, 0.0), axis=1, keepdims=True
    ).reshape(V, K, 1)
    pturn[...] = chosen.T[64:96].astype(BF16)
    send_plane(lambda chip: pturn, recvp.at[p], 4)
    recvp[p] = pturn[...]

    whole(recvf.at[pl.ds(0, 15)], 3).wait_recv()
    pixels = recvf[...].reshape(TOK, VK).astype(F32).T.reshape(V, K, TOK)
    scores = jnp.sum(pixels * key_rows, axis=1) + key_bias
    exponent = jnp.exp(scores)
    attention = exponent / jnp.sum(exponent, axis=0, keepdims=True)
    weighted = pixels * attention[:, None, :]
    aa[pl.ds(0, VK)] = weighted.reshape(VK, TOK).astype(BF16)
    aa[pl.ds(VK, V)] = attention.astype(BF16)
    whole(recvh.at[pl.ds(0, 15)], 2).wait_recv()
    grads = recvh[...].reshape(TOK, 128)
    head_weights = mm[...].reshape(VK + V, 128)
    lhs = aa[...]
    sums = dot(lhs, grads)
    cross = dot(head_weights, grads, 1, 1)
    dweights = jnp.sum(pixels * cross[0:VK].reshape(V, K, TOK), axis=1) + cross[VK : VK + V]
    dscores = attention * (
        dweights - jnp.sum(attention * dweights, axis=0, keepdims=True)
    )
    score_sums = jnp.sum(pixels * dscores[:, None, :], axis=2, keepdims=True)
    score_rows = jnp.sum(jnp.where(lane16 == 64 + row16, score_sums, 0.0), axis=1)
    dense = sums[0:128] + pltpu.roll(sums[128:256], 64, 1)
    gtile[pl.ds(0, 8)] = dense.astype(BF16).reshape(8, 16, 128)
    gtile[8] = (sums[VK : VK + V] + score_rows).astype(BF16)

    for d in range(1, 8):
        j = lax.rem(own_j + d, 8)
        send(gtile.at[j], recvr.at[own_j], 5, quad_device(j))
    recvr[own_j] = gtile[own_j]
    has_bias = own_j == 1

    @pl.when(has_bias)
    def _():
        recvb[own_j] = gtile[8]

    @pl.when(jnp.logical_not(has_bias))
    def _():
        send(gtile.at[8], recvb.at[own_j], 6, quad_device(jnp.int32(1)))

    pooled = dot(lhs, head_weights, 0, 0)
    pmsg[...] = pooled.astype(BF16).reshape(NP, T, 128)

    whole(recvr.at[pl.ds(0, 7)], 5).wait_recv()
    quad[...] = jnp.sum(recvr[...].astype(F32), axis=0).astype(BF16)
    for d in FAR_FIRST:
        send(quad, recvq.at[z], 10, zpeer(d))
    recvq[z] = quad[...]

    @pl.when(has_bias)
    def _():
        whole(recvb.at[pl.ds(0, 7)], 6).wait_recv()
        quadb[...] = jnp.sum(recvb[...].astype(F32), axis=0).astype(BF16)
        for d in FAR_FIRST:
            send(quadb, recvqb.at[z // 4], 11, zpeer(d))
        recvqb[z // 4] = quadb[...]

    send_plane(lambda chip: pmsg.at[chip], recvpool.at[p], 7)
    recvpool[p] = pmsg[p]

    whole(recvp.at[pl.ds(0, 15)], 4).wait_recv()
    whole(recvq.at[pl.ds(0, 15)], 10).wait_recv()
    half = jnp.sum(recvq[...].astype(F32).reshape(4, 4, 16, 128), axis=0).astype(BF16)
    half_at = pl.multiple_of(5 * core, 5)
    gtot[pl.ds(half_at, 4)] = half

    @pl.when(core == 1)
    def _():
        gtot[9] = jnp.zeros((16, 128), BF16)

    @pl.when((core == 0) & has_bias)
    def _():
        whole(recvqb.at[pl.ds(0, 3)], 11).wait_recv()

    @pl.when((core == 0) & jnp.logical_not(has_bias))
    def _():
        whole(recvqb, 11).wait_recv()

    @pl.when(core == 0)
    def _():
        gtot[4] = jnp.sum(recvqb[...].astype(F32), axis=0).astype(BF16)

    send(gtot.at[pl.ds(half_at, 5)], gtot.at[pl.ds(half_at, 5)], 12, sibling)
    whole(gtot.at[pl.ds(0, 5)], 12).wait_recv()

    bias_rows = pwve[pl.ds(32, 16)]
    rows_all = recvp[...].reshape(TOK, VK)
    patch_sums = jnp.concatenate([gtot[pl.ds(0, 4)], gtot[pl.ds(5, 4)]], axis=0).reshape(128, 128)
    bias_sums = gtot[4]
    low = dot(rows_all[:, 0:128], patch_sums)
    high = dot(rows_all[:, 128:256], patch_sums)
    bias_all = dot(bias_rows, bias_sums, 0, 0).reshape(NP, 2, T, 128)
    bias = jnp.where(core == 0, bias_all[:, 0], bias_all[:, 1])
    value_rows = (low + pltpu.roll(high, 64, 1)).reshape(NP, T, 128) + bias
    picked, score_parts = [], []
    for s in range(2):
        var_of, has = held[s]
        at = lax.rem(var_of, 8)
        tile = gtot[at + at // 4].astype(F32)
        tile = jnp.where(var_of < 8, pltpu.roll(tile, 64, 1), tile)
        picked.append(tile * has.astype(F32))
        line = jnp.where((row16 == var_of) & (lane16 >= 64) & (lane16 < 80), bias_sums.astype(F32), 0.0)
        line = jnp.sum(line, axis=0, keepdims=True) * has.astype(F32)
        score_parts.append(pltpu.roll(line, 64 + 16 * s, 1))
    mine = jnp.concatenate(picked, axis=0)
    score_line = jnp.broadcast_to(score_parts[0] + score_parts[1], (16, 128)).astype(BF16)
    msg5[:, 0:32, :] = jnp.where(lane32 < 64, value_rows, mine).astype(BF16)
    msg5[:, 32:48, :] = jnp.broadcast_to(score_line, (NP, 16, 128))
    for step in PLANE_STEPS:
        chip = plane_chip(step)
        slot = {0: 8, 1: 9, 3: 9, 2: 13}[step[0]]
        send(msg5.at[chip], recv5.at[p], slot, plane_peer(chip))
    recv5[p] = msg5[p]

    whole(recvpool.at[pl.ds(0, 15)], 7).wait_recv()
    parts = []
    for q in range(8):
        left = recvpool[2 * q].astype(F32)
        right = recvpool[2 * q + 1].astype(F32)
        parts.append(jnp.where(lane32 < 64, left, pltpu.roll(right, 64, 1)).astype(BF16))
    projected = dot(jnp.concatenate(parts, axis=1), ow_v[...])
    agg_ref[...] = (projected * valid).astype(BF16)

    loads[7].wait()
    patch_grad = jnp.zeros((32, D), F32)
    score_lines = jnp.zeros((16, 128), F32)
    for i, dx in enumerate((0, 1, 3, 2)):
        if i == 0:
            whole(recv5.at[pl.ds(0, 3)], 8).wait_recv()
        if i == 1:
            whole(recv5.at[pl.ds(0, 8)], 9).wait_recv()
        if i == 3:
            whole(recv5.at[pl.ds(0, 4)], 13).wait_recv()
        row = lax.rem(x + dx, 4)
        parts = []
        for q in range(2):
            left = recv5[4 * row + 2 * q, 0:32].astype(F32)
            right = recv5[4 * row + 2 * q + 1, 0:32].astype(F32)
            at = pl.multiple_of(256 * row + 128 * q, 128)
            dvw_ref[:, pl.ds(at, 128)] = jnp.where(lane32 < 64, left, pltpu.roll(right, 64, 1))
            parts.append(jnp.where(lane32 < 64, pltpu.roll(left, 64, 1), right).astype(BF16))
        columns = vw_v[:, pl.ds(pl.multiple_of(256 * row, 256), 256)]
        patch_grad = patch_grad + dot(jnp.concatenate(parts, axis=1), columns, 1, 1)
        for q in range(4):
            line = recv5[4 * row + q, 32:48].astype(F32)
            score_lines = jnp.where(row16 == 4 * row + q, line, score_lines)
    score_grad = score_lines.T[0:32].astype(BF16)
    dpw_ref[...] = patch_grad + dot(score_grad, kq_v[...])

    whole(recv0.at[pl.ds(0, 15)], 0).wait_send()
    whole(recv1.at[pl.ds(0, 30)], 1).wait_send()
    whole(recvh.at[pl.ds(0, 15)], 2).wait_send()
    whole(recvf.at[pl.ds(0, 15)], 3).wait_send()
    whole(recvp.at[pl.ds(0, 15)], 4).wait_send()
    whole(recvr.at[pl.ds(0, 7)], 5).wait_send()
    whole(recvpool.at[pl.ds(0, 15)], 7).wait_send()
    whole(recv5.at[pl.ds(0, 3)], 8).wait_send()
    whole(recv5.at[pl.ds(0, 8)], 9).wait_send()
    whole(recv5.at[pl.ds(0, 4)], 13).wait_send()
    whole(recvq.at[pl.ds(0, 15)], 10).wait_send()
    whole(gtot.at[pl.ds(0, 5)], 12).wait_send()

    @pl.when(has_bias)
    def _():
        whole(recvq.at[pl.ds(0, 15)], 11).wait_send()

    @pl.when(jnp.logical_not(has_bias))
    def _():
        whole(quadb, 6).wait_send()


def place_kernel(*refs):
    sources, results, sems = refs[:3], refs[3:6], refs[6]
    stores = [pltpu.make_async_copy(sources[i], results[i], sems.at[i]) for i in range(3)]
    for store in stores:
        store.start()
    for store in stores:
        store.wait()


def per_device(
    fields,
    owner_table,
    band_tokens,
    patch_weight,
    var_embed,
    key_query,
    value_weight,
    out_weight,
    cotangent,
):
    hbm_spec = pl.BlockSpec(memory_space=pltpu.HBM)
    vmem_spec = pl.BlockSpec(memory_space=pltpu.VMEM)
    aggregated, value_grad, patch_grad = pl.pallas_call(
        pooling_kernel,
        out_shape=(
            pltpu.VMEM((T, D), BF16),
            pltpu.VMEM((32, D), F32),
            pltpu.VMEM((32, D), F32),
        ),
        in_specs=[hbm_spec] * 9,
        out_specs=(vmem_spec, vmem_spec, vmem_spec),
        scratch_shapes=[
            pltpu.SMEM((V,), jnp.int32),
            pltpu.SMEM((2 * NP,), jnp.int32),
            pltpu.VMEM((2, K, 512), BF16),
            pltpu.VMEM((48, D), BF16),
            pltpu.VMEM((16, D), BF16),
            pltpu.VMEM((D, 128), BF16),
            pltpu.VMEM((D, D), BF16),
            pltpu.VMEM((D, D), BF16),
            pltpu.VMEM((T, D), BF16),
            pltpu.VMEM((NZ, K, 128), BF16),
            pltpu.VMEM((NZ, K, 128), BF16),
            pltpu.VMEM((2, K, 128), BF16),
            pltpu.VMEM((2 * NZ, K, 128), BF16),
            pltpu.VMEM((NP, T, 128), BF16),
            pltpu.VMEM((NP, T, 128), BF16),
            pltpu.VMEM((V + 1, K, 128), BF16),
            pltpu.VMEM((T, VK), BF16),
            pltpu.VMEM((32, VK), BF16),
            pltpu.VMEM((NP, T, VK), BF16),
            pltpu.VMEM((NP, T, VK), BF16),
            pltpu.VMEM((VK + V, TOK), BF16),
            pltpu.VMEM((NP, T, 128), BF16),
            pltpu.VMEM((NP, T, 128), BF16),
            pltpu.VMEM((TILES, 16, 128), BF16),
            pltpu.VMEM((8, 16, 128), BF16),
            pltpu.VMEM((8, 16, 128), BF16),
            pltpu.VMEM((16, 128), BF16),
            pltpu.VMEM((16, 128), BF16),
            pltpu.VMEM((NZ, 16, 128), BF16),
            pltpu.VMEM((4, 16, 128), BF16),
            pltpu.VMEM((10, 16, 128), BF16),
            pltpu.VMEM((NP, 48, 128), BF16),
            pltpu.VMEM((NP, 48, 128), BF16),
            pltpu.SemaphoreType.DMA((10,)),
            pltpu.SemaphoreType.DMA((14,)),
            pltpu.SemaphoreType.DMA((14,)),
        ],
        compiler_params=pltpu.CompilerParams(
            collective_id=0, has_side_effects=True, vmem_limit_bytes=60 * 1024 * 1024
        ),
        cost_estimate=pl.CostEstimate(
            flops=2_000_000_000, bytes_accessed=5_000_000, transcendentals=8192
        ),
    )(
        owner_table,
        band_tokens,
        fields,
        patch_weight.reshape(32, D),
        var_embed,
        key_query.T,
        value_weight,
        out_weight,
        cotangent.reshape(T, D),
    )
    aggregated, value_grad, patch_grad = pl.pallas_call(
        place_kernel,
        out_shape=(
            jax.ShapeDtypeStruct((T, D), BF16),
            jax.ShapeDtypeStruct((32, D), F32),
            jax.ShapeDtypeStruct((32, D), F32),
        ),
        in_specs=[hbm_spec] * 3,
        out_specs=(hbm_spec,) * 3,
        scratch_shapes=[pltpu.SemaphoreType.DMA((3,))],
        compiler_params=pltpu.CompilerParams(vmem_limit_bytes=4 * 1024 * 1024),
    )(aggregated, value_grad, patch_grad)
    return (
        aggregated.reshape(1, T, D),
        value_grad,
        patch_grad.reshape(2, K, D),
    )


def solution(mesh):
    in_specs = (
        P("var", None, "lat"),
        P(),
        P(),
        P("var", None, None),
        P(),
        P(),
        P(),
        P(),
        P("lat", "var", None),
    )
    out_specs = (P("lat", "var", None), P("lat", None), P("var", None, None))
    return jax.shard_map(
        per_device, mesh=mesh, in_specs=in_specs, out_specs=out_specs, check_vma=False
    )
```

```python
import functools

import jax
import jax.numpy as jnp
from jax import lax
from jax.experimental import pallas as pl
from jax.experimental.pallas import tpu as pltpu
from jax.sharding import PartitionSpec as P

MESH = pl.DeviceIdType.MESH
F32 = jnp.float32
BF16 = jnp.bfloat16

NZ = 16
NP = 16
V = 16
K = 16
T = 32
D = 1024
DIRECT = 2
TILES = 9
FAR_FIRST = (8, 7, 9, 6, 10, 5, 11, 4, 12, 3, 13, 2, 14, 1, 15)
PLANE_STEPS = sorted(
    [(dx, dy) for dx in range(4) for dy in range(4) if dx or dy],
    key=lambda step: -sum(min(d, 4 - d) for d in step),
)
VK = V * K
TOK = NP * T


def dot(a, b, ca=1, cb=0):
    return lax.dot_general(a, b, (((ca,), (cb,)), ((), ())), preferred_element_type=F32)


def pooling_kernel(
    owner_hbm,
    band_hbm,
    fields_hbm,
    pw_hbm,
    ve_hbm,
    kq_hbm,
    vw_hbm,
    ow_hbm,
    cot_hbm,
    agg_ref,
    dvw_ref,
    dpw_ref,
    owner_ref,
    band_ref,
    fields_v,
    pwve,
    kq_v,
    vwg,
    vw_v,
    ow_v,
    cot_v,
    fmsg,
    recv0,
    wmsg,
    recv1,
    hmsg,
    recvh,
    mm,
    fturn,
    pturn,
    recvf,
    recvp,
    aa,
    pmsg,
    recvpool,
    gtile,
    recvr,
    recvb,
    quad,
    quadb,
    recvq,
    recvx,
    recvqb,
    gtot,
    msg5,
    recv5,
    load_sem,
    send_sem,
    recv_sem,
):
    z = lax.axis_index("var")
    lat = lax.axis_index("lat")
    core = lax.rem(lat, 2)
    p = lat // 2

    x, y = p // 4, lax.rem(p, 4)
    sibling = {"var": z, "lat": p * 2 + 1 - core}

    def zpeer(d):
        return {"var": lax.rem(z + d, NZ), "lat": lat}

    def other_core(zt):
        return {"var": zt, "lat": p * 2 + 1 - core}

    def plane_chip(step):
        return lax.rem(x + step[0], 4) * 4 + lax.rem(y + step[1], 4)

    def plane_peer(chip):
        return {"var": z, "lat": chip * 2 + core}

    def quad_device(j):
        return {"var": (z // 4) * 4 + lax.rem(j, 4), "lat": p * 2 + j // 4}

    barrier = pltpu.get_barrier_semaphore()

    def signal(device):
        pl.semaphore_signal(barrier, inc=1, device_id=device, device_id_type=MESH)

    own_j = core * 4 + lax.rem(z, 4)
    for d in FAR_FIRST:
        signal(zpeer(d))

    @pl.when(z < DIRECT)
    def _():
        for d in FAR_FIRST:
            signal(other_core(lax.rem(z + d, NZ)))

    @pl.when(z >= DIRECT)
    def _():
        for d in range(1, 4):
            signal(other_core((z // 4) * 4 + lax.rem(z + d, 4)))

    for step in PLANE_STEPS:
        signal(plane_peer(plane_chip(step)))
    signal(sibling)
    def whole(ref, slot):
        return pltpu.make_async_remote_copy(
            src_ref=ref,
            dst_ref=ref,
            send_sem=send_sem.at[slot],
            recv_sem=recv_sem.at[slot],
            device_id=sibling,
            device_id_type=MESH,
        )

    def send(src, dst, slot, device):
        pltpu.make_async_remote_copy(
            src_ref=src,
            dst_ref=dst,
            send_sem=send_sem.at[slot],
            recv_sem=recv_sem.at[slot],
            device_id=device,
            device_id_type=MESH,
        ).start()

    def send_plane(src, dst, slot):
        for step in PLANE_STEPS:
            chip = plane_chip(step)
            send(src(chip), dst, slot, plane_peer(chip))

    group = pl.multiple_of((p // 2) * 128, 128)
    loads = [
        pltpu.make_async_copy(fields_hbm, fields_v, load_sem.at[4]),
        pltpu.make_async_copy(pw_hbm, pwve.at[pl.ds(0, 32)], load_sem.at[0]),
        pltpu.make_async_copy(ve_hbm, pwve.at[pl.ds(32, 16)], load_sem.at[1]),
        pltpu.make_async_copy(vw_hbm.at[:, pl.ds(group, 128)], vwg, load_sem.at[2]),
        pltpu.make_async_copy(kq_hbm, kq_v, load_sem.at[3]),
        pltpu.make_async_copy(cot_hbm, cot_v, load_sem.at[5]),
        pltpu.make_async_copy(ow_hbm, ow_v, load_sem.at[6]),
        pltpu.make_async_copy(vw_hbm, vw_v, load_sem.at[7]),
        pltpu.make_async_copy(owner_hbm, owner_ref, load_sem.at[8]),
        pltpu.make_async_copy(band_hbm, band_ref, load_sem.at[9]),
    ]
    for load in loads[8:] + loads[:8]:
        load.start()

    lane16 = lax.broadcasted_iota(jnp.int32, (16, 128), 1)
    row16 = lax.broadcasted_iota(jnp.int32, (16, 128), 0)
    lane32 = lax.broadcasted_iota(jnp.int32, (32, 128), 1)
    loads[0].wait()
    for q in range(4):
        low = fields_v[0, :, 128 * q : 128 * q + 128].astype(F32)
        high = fields_v[1, :, 128 * q : 128 * q + 128].astype(F32)
        for r in range(4):
            left = pltpu.roll(low, (128 - 32 * r) % 128, 1) if r else low
            right = pltpu.roll(high, (160 - 32 * r) % 128, 1) if r != 1 else high
            piece = jnp.where(lane16 < 32, left, jnp.where(lane16 < 64, right, 0.0))
            fmsg[4 * q + r] = piece.astype(BF16)

    loads[8].wait()
    owners = [owner_ref[v] for v in range(V)]
    slots = []
    for v in range(V):
        rank = jnp.int32(0)
        for u in range(v):
            rank = rank + (owners[u] == owners[v]).astype(jnp.int32)
        slots.append(owners[v] * 2 + rank)
    held = []
    for s in range(2):
        var_of, has = jnp.int32(0), jnp.int32(0)
        for v in range(V):
            hit = (slots[v] == 2 * z + s).astype(jnp.int32)
            var_of, has = var_of + hit * v, has + hit
        held.append((var_of, has))

    for i in range(1, 5):
        loads[i].wait()
    turn = lax.rem(p, 2) * 64
    both = pwve[...]
    head_cols = pltpu.roll(dot(both, vwg[...]), turn, 1)
    key_cols = dot(both, kq_v[...], 1, 1)
    key_lane = lax.broadcasted_iota(jnp.int32, (48, 16), 1)
    key_col = jnp.sum(jnp.where(key_lane == p, key_cols, 0.0), axis=1, keepdims=True)
    key_bias = key_col[32:48]
    mm[V] = jnp.where(lane16 < 64, head_cols[32:48], 0.0).astype(BF16)
    own_group = pl.multiple_of((lat // 4) * 128, 128)
    own_cols = pltpu.roll(
        pwve[pl.ds(0, 32), pl.ds(own_group, 128)].astype(F32),
        lax.rem(192 - 32 * lax.rem(lat, 4), 128),
        1,
    )
    key_top = key_col[0:32].astype(BF16).astype(F32)
    key_mid = (key_col[0:32] - key_top).astype(BF16).astype(F32)
    key_low = key_col[0:32] - key_top - key_mid
    packed = jnp.where(lane32 < 64, head_cols[0:32], own_cols)
    packed = jnp.where(lane32 < 96, packed, jnp.where(lane32 == 96, key_top, 0.0))
    packed = jnp.where(lane32 == 97, key_mid, jnp.where(lane32 == 98, key_low, packed))
    wmsg[...] = packed.astype(BF16).reshape(2, 16, 128)

    pl.semaphore_wait(barrier, jnp.where(z < 4, 34, 34 + DIRECT))

    for d in FAR_FIRST:
        send(fmsg.at[lax.rem(z + d, NZ)], recv0.at[z], 0, zpeer(d))
    for d in FAR_FIRST:
        send(wmsg, recv1.at[pl.ds(2 * z, 2)], 1, zpeer(d))
    recv0[z] = fmsg[z]
    recv1[pl.ds(2 * z, 2)] = wmsg[...]

    loads[5].wait()
    loads[9].wait()
    count = band_ref[lat]
    rows = z * T + lax.broadcasted_iota(jnp.int32, (T, 1), 0)
    valid = (rows < count).astype(F32)
    masked = (cot_v[...].astype(F32) * valid).astype(BF16)
    loads[6].wait()
    head_grads = dot(masked, ow_v[...], 1, 1)
    for q in range(8):
        two = head_grads[:, 128 * q : 128 * q + 128]
        hmsg[2 * q] = jnp.where(lane32 < 64, two, 0.0).astype(BF16)
        hmsg[2 * q + 1] = jnp.where(lane32 < 64, pltpu.roll(two, 64, 1), 0.0).astype(BF16)

    send_plane(lambda chip: hmsg.at[chip], recvh.at[p], 2)
    recvh[p] = hmsg[p]

    whole(recv0.at[pl.ds(0, 15)], 0).wait_recv()
    pieces = []
    for v in range(V):
        tile = recv0[slots[v] // 2].astype(F32)
        pieces.append(pltpu.roll(tile, lax.rem(128 - 32 * lax.rem(slots[v], 2), 128), 1))
    fturn[...] = jnp.concatenate(pieces, axis=0).T[0:32].astype(BF16)
    send_plane(lambda chip: fturn, recvf.at[p], 3)
    recvf[p] = fturn[...]

    whole(recv1.at[pl.ds(0, 30)], 1).wait_recv()
    for v in range(V):
        mm[v] = recv1[slots[v]]
    chosen = mm[pl.ds(0, V)].reshape(VK, 128).astype(F32)
    lane_all = lax.broadcasted_iota(jnp.int32, (VK, 128), 1)
    key_rows = jnp.sum(
        jnp.where((lane_all >= 96) & (lane_all < 99), chosen, 0.0), axis=1, keepdims=True
    ).reshape(V, K, 1)
    pturn[...] = chosen.T[64:96].astype(BF16)
    send_plane(lambda chip: pturn, recvp.at[p], 4)
    recvp[p] = pturn[...]

    whole(recvf.at[pl.ds(0, 15)], 3).wait_recv()
    pixels = recvf[...].reshape(TOK, VK).astype(F32).T.reshape(V, K, TOK)
    scores = jnp.sum(pixels * key_rows, axis=1) + key_bias
    exponent = jnp.exp(scores)
    attention = exponent / jnp.sum(exponent, axis=0, keepdims=True)
    weighted = pixels * attention[:, None, :]
    aa[pl.ds(0, VK)] = weighted.reshape(VK, TOK).astype(BF16)
    aa[pl.ds(VK, V)] = attention.astype(BF16)
    whole(recvh.at[pl.ds(0, 15)], 2).wait_recv()
    grads = recvh[...].reshape(TOK, 128)
    head_weights = mm[...].reshape(VK + V, 128)
    lhs = aa[...]
    sums = dot(lhs, grads)
    cross = dot(head_weights, grads, 1, 1)
    dweights = jnp.sum(pixels * cross[0:VK].reshape(V, K, TOK), axis=1) + cross[VK : VK + V]
    dscores = attention * (
        dweights - jnp.sum(attention * dweights, axis=0, keepdims=True)
    )
    score_sums = jnp.sum(pixels * dscores[:, None, :], axis=2, keepdims=True)
    score_rows = jnp.sum(jnp.where(lane16 == 64 + row16, score_sums, 0.0), axis=1)
    dense = sums[0:128] + pltpu.roll(sums[128:256], 64, 1)
    gtile[pl.ds(0, 8)] = dense.astype(BF16).reshape(8, 16, 128)
    gtile[8] = (sums[VK : VK + V] + score_rows).astype(BF16)

    for d in range(1, 8):
        j = lax.rem(own_j + d, 8)
        send(gtile.at[j], recvr.at[own_j], 5, quad_device(j))
    recvr[own_j] = gtile[own_j]
    has_bias = own_j == 1

    @pl.when(has_bias)
    def _():
        recvb[own_j] = gtile[8]

    @pl.when(jnp.logical_not(has_bias))
    def _():
        send(gtile.at[8], recvb.at[own_j], 6, quad_device(jnp.int32(1)))

    pooled = dot(lhs, head_weights, 0, 0)
    pmsg[...] = pooled.astype(BF16).reshape(NP, T, 128)

    whole(recvr.at[pl.ds(0, 7)], 5).wait_recv()
    quad[...] = jnp.sum(recvr[...].astype(F32), axis=0).astype(BF16)
    for zt in range(DIRECT):
        send(quad, recvx.at[z], 14, other_core(zt))
    for d in FAR_FIRST:
        send(quad, recvq.at[z], 10, zpeer(d))
    recvq[z] = quad[...]

    @pl.when(has_bias)
    def _():
        whole(recvb.at[pl.ds(0, 7)], 6).wait_recv()
        quadb[...] = jnp.sum(recvb[...].astype(F32), axis=0).astype(BF16)
        for zt in range(DIRECT):
            send(quadb, recvqb.at[z // 4], 11, other_core(zt))
        for d in FAR_FIRST:
            send(quadb, recvqb.at[z // 4], 11, zpeer(d))
        recvqb[z // 4] = quadb[...]

    send_plane(lambda chip: pmsg.at[chip], recvpool.at[p], 7)
    recvpool[p] = pmsg[p]

    whole(recvp.at[pl.ds(0, 15)], 4).wait_recv()
    whole(recvq.at[pl.ds(0, 15)], 10).wait_recv()
    half_at = pl.multiple_of(5 * core, 5)
    rest_at = pl.multiple_of(5 - 5 * core, 5)
    direct = z < DIRECT

    def four_tiles(ref):
        return jnp.sum(ref[...].astype(F32).reshape(4, 4, 16, 128), axis=0).astype(BF16)

    gtot[pl.ds(half_at, 4)] = four_tiles(recvq)

    @pl.when((core == 0) & has_bias)
    def _():
        whole(recvqb.at[pl.ds(0, 3)], 11).wait_recv()

    @pl.when(((core == 0) & jnp.logical_not(has_bias)) | ((core == 1) & direct))
    def _():
        whole(recvqb, 11).wait_recv()

    @pl.when((core == 0) | direct)
    def _():
        gtot[4] = jnp.sum(recvqb[...].astype(F32), axis=0).astype(BF16)

    @pl.when((core == 1) & jnp.logical_not(direct))
    def _():
        gtot[9] = jnp.zeros((16, 128), BF16)

    @pl.when(direct)
    def _():
        whole(recvx, 14).wait_recv()
        gtot[pl.ds(rest_at, 4)] = four_tiles(recvx)

    @pl.when(jnp.logical_not(direct))
    def _():
        send(gtot.at[pl.ds(half_at, 5)], gtot.at[pl.ds(half_at, 5)], 12, sibling)
        whole(gtot.at[pl.ds(0, 5)], 12).wait_recv()

    bias_rows = pwve[pl.ds(32, 16)]
    rows_all = recvp[...].reshape(TOK, VK)
    patch_sums = jnp.concatenate([gtot[pl.ds(0, 4)], gtot[pl.ds(5, 4)]], axis=0).reshape(128, 128)
    bias_sums = gtot[4]
    low = dot(rows_all[:, 0:128], patch_sums)
    high = dot(rows_all[:, 128:256], patch_sums)
    bias_all = dot(bias_rows, bias_sums, 0, 0).reshape(NP, 2, T, 128)
    bias = jnp.where(core == 0, bias_all[:, 0], bias_all[:, 1])
    value_rows = (low + pltpu.roll(high, 64, 1)).reshape(NP, T, 128) + bias
    picked, score_parts = [], []
    for s in range(2):
        var_of, has = held[s]
        at = lax.rem(var_of, 8)
        tile = gtot[at + at // 4].astype(F32)
        tile = jnp.where(var_of < 8, pltpu.roll(tile, 64, 1), tile)
        picked.append(tile * has.astype(F32))
        line = jnp.where((row16 == var_of) & (lane16 >= 64) & (lane16 < 80), bias_sums.astype(F32), 0.0)
        line = jnp.sum(line, axis=0, keepdims=True) * has.astype(F32)
        score_parts.append(pltpu.roll(line, 64 + 16 * s, 1))
    mine = jnp.concatenate(picked, axis=0)
    score_line = jnp.broadcast_to(score_parts[0] + score_parts[1], (16, 128)).astype(BF16)
    msg5[:, 0:32, :] = jnp.where(lane32 < 64, value_rows, mine).astype(BF16)
    msg5[:, 32:48, :] = jnp.broadcast_to(score_line, (NP, 16, 128))
    for step in PLANE_STEPS:
        chip = plane_chip(step)
        slot = {0: 8, 1: 9, 3: 9, 2: 13}[step[0]]
        send(msg5.at[chip], recv5.at[p], slot, plane_peer(chip))
    recv5[p] = msg5[p]

    whole(recvpool.at[pl.ds(0, 15)], 7).wait_recv()
    parts = []
    for q in range(8):
        left = recvpool[2 * q].astype(F32)
        right = recvpool[2 * q + 1].astype(F32)
        parts.append(jnp.where(lane32 < 64, left, pltpu.roll(right, 64, 1)).astype(BF16))
    projected = dot(jnp.concatenate(parts, axis=1), ow_v[...])
    agg_ref[...] = (projected * valid).astype(BF16)

    loads[7].wait()
    patch_grad = jnp.zeros((32, D), F32)
    score_lines = jnp.zeros((16, 128), F32)
    for i, dx in enumerate((0, 1, 3, 2)):
        if i == 0:
            whole(recv5.at[pl.ds(0, 3)], 8).wait_recv()
        if i == 1:
            whole(recv5.at[pl.ds(0, 8)], 9).wait_recv()
        if i == 3:
            whole(recv5.at[pl.ds(0, 4)], 13).wait_recv()
        row = lax.rem(x + dx, 4)
        parts = []
        for q in range(2):
            left = recv5[4 * row + 2 * q, 0:32].astype(F32)
            right = recv5[4 * row + 2 * q + 1, 0:32].astype(F32)
            at = pl.multiple_of(256 * row + 128 * q, 128)
            dvw_ref[:, pl.ds(at, 128)] = jnp.where(lane32 < 64, left, pltpu.roll(right, 64, 1))
            parts.append(jnp.where(lane32 < 64, pltpu.roll(left, 64, 1), right).astype(BF16))
        columns = vw_v[:, pl.ds(pl.multiple_of(256 * row, 256), 256)]
        patch_grad = patch_grad + dot(jnp.concatenate(parts, axis=1), columns, 1, 1)
        for q in range(4):
            line = recv5[4 * row + q, 32:48].astype(F32)
            score_lines = jnp.where(row16 == 4 * row + q, line, score_lines)
    score_grad = score_lines.T[0:32].astype(BF16)
    dpw_ref[...] = patch_grad + dot(score_grad, kq_v[...])

    whole(recv0.at[pl.ds(0, 15)], 0).wait_send()
    whole(recv1.at[pl.ds(0, 30)], 1).wait_send()
    whole(recvh.at[pl.ds(0, 15)], 2).wait_send()
    whole(recvf.at[pl.ds(0, 15)], 3).wait_send()
    whole(recvp.at[pl.ds(0, 15)], 4).wait_send()
    whole(recvr.at[pl.ds(0, 7)], 5).wait_send()
    whole(recvpool.at[pl.ds(0, 15)], 7).wait_send()
    whole(recv5.at[pl.ds(0, 3)], 8).wait_send()
    whole(recv5.at[pl.ds(0, 8)], 9).wait_send()
    whole(recv5.at[pl.ds(0, 4)], 13).wait_send()
    whole(recvq.at[pl.ds(0, 15)], 10).wait_send()
    whole(recvx.at[pl.ds(0, DIRECT)], 14).wait_send()

    @pl.when(jnp.logical_not(direct))
    def _():
        whole(gtot.at[pl.ds(0, 5)], 12).wait_send()


    @pl.when(has_bias)
    def _():
        whole(recv1.at[pl.ds(0, 15 + DIRECT)], 11).wait_send()

    @pl.when(jnp.logical_not(has_bias))
    def _():
        whole(quadb, 6).wait_send()


def place_kernel(*refs):
    sources, results, sems = refs[:3], refs[3:6], refs[6]
    stores = [pltpu.make_async_copy(sources[i], results[i], sems.at[i]) for i in range(3)]
    for store in stores:
        store.start()
    for store in stores:
        store.wait()


def per_device(
    fields,
    owner_table,
    band_tokens,
    patch_weight,
    var_embed,
    key_query,
    value_weight,
    out_weight,
    cotangent,
):
    hbm_spec = pl.BlockSpec(memory_space=pltpu.HBM)
    vmem_spec = pl.BlockSpec(memory_space=pltpu.VMEM)
    aggregated, value_grad, patch_grad = pl.pallas_call(
        pooling_kernel,
        out_shape=(
            pltpu.VMEM((T, D), BF16),
            pltpu.VMEM((32, D), F32),
            pltpu.VMEM((32, D), F32),
        ),
        in_specs=[hbm_spec] * 9,
        out_specs=(vmem_spec, vmem_spec, vmem_spec),
        scratch_shapes=[
            pltpu.SMEM((V,), jnp.int32),
            pltpu.SMEM((2 * NP,), jnp.int32),
            pltpu.VMEM((2, K, 512), BF16),
            pltpu.VMEM((48, D), BF16),
            pltpu.VMEM((16, D), BF16),
            pltpu.VMEM((D, 128), BF16),
            pltpu.VMEM((D, D), BF16),
            pltpu.VMEM((D, D), BF16),
            pltpu.VMEM((T, D), BF16),
            pltpu.VMEM((NZ, K, 128), BF16),
            pltpu.VMEM((NZ, K, 128), BF16),
            pltpu.VMEM((2, K, 128), BF16),
            pltpu.VMEM((2 * NZ, K, 128), BF16),
            pltpu.VMEM((NP, T, 128), BF16),
            pltpu.VMEM((NP, T, 128), BF16),
            pltpu.VMEM((V + 1, K, 128), BF16),
            pltpu.VMEM((T, VK), BF16),
            pltpu.VMEM((32, VK), BF16),
            pltpu.VMEM((NP, T, VK), BF16),
            pltpu.VMEM((NP, T, VK), BF16),
            pltpu.VMEM((VK + V, TOK), BF16),
            pltpu.VMEM((NP, T, 128), BF16),
            pltpu.VMEM((NP, T, 128), BF16),
            pltpu.VMEM((TILES, 16, 128), BF16),
            pltpu.VMEM((8, 16, 128), BF16),
            pltpu.VMEM((8, 16, 128), BF16),
            pltpu.VMEM((16, 128), BF16),
            pltpu.VMEM((16, 128), BF16),
            pltpu.VMEM((NZ, 16, 128), BF16),
            pltpu.VMEM((NZ, 16, 128), BF16),
            pltpu.VMEM((4, 16, 128), BF16),
            pltpu.VMEM((10, 16, 128), BF16),
            pltpu.VMEM((NP, 48, 128), BF16),
            pltpu.VMEM((NP, 48, 128), BF16),
            pltpu.SemaphoreType.DMA((10,)),
            pltpu.SemaphoreType.DMA((15,)),
            pltpu.SemaphoreType.DMA((15,)),
        ],
        compiler_params=pltpu.CompilerParams(
            collective_id=0, has_side_effects=True, vmem_limit_bytes=60 * 1024 * 1024
        ),
        cost_estimate=pl.CostEstimate(
            flops=2_000_000_000, bytes_accessed=5_000_000, transcendentals=8192
        ),
    )(
        owner_table,
        band_tokens,
        fields,
        patch_weight.reshape(32, D),
        var_embed,
        key_query.T,
        value_weight,
        out_weight,
        cotangent.reshape(T, D),
    )
    aggregated, value_grad, patch_grad = pl.pallas_call(
        place_kernel,
        out_shape=(
            jax.ShapeDtypeStruct((T, D), BF16),
            jax.ShapeDtypeStruct((32, D), F32),
            jax.ShapeDtypeStruct((32, D), F32),
        ),
        in_specs=[hbm_spec] * 3,
        out_specs=(hbm_spec,) * 3,
        scratch_shapes=[pltpu.SemaphoreType.DMA((3,))],
        compiler_params=pltpu.CompilerParams(vmem_limit_bytes=4 * 1024 * 1024),
    )(aggregated, value_grad, patch_grad)
    return (
        aggregated.reshape(1, T, D),
        value_grad,
        patch_grad.reshape(2, K, D),
    )


def solution(mesh):
    in_specs = (
        P("var", None, "lat"),
        P(),
        P(),
        P("var", None, None),
        P(),
        P(),
        P(),
        P(),
        P("lat", "var", None),
    )
    out_specs = (P("lat", "var", None), P("lat", None), P("var", None, None))
    return jax.shard_map(
        per_device, mesh=mesh, in_specs=in_specs, out_specs=out_specs, check_vma=False
    )
```

```python
import functools

import jax
import jax.numpy as jnp
from jax import lax
from jax.experimental import pallas as pl
from jax.experimental.pallas import tpu as pltpu
from jax.sharding import PartitionSpec as P

MESH = pl.DeviceIdType.MESH
F32 = jnp.float32
BF16 = jnp.bfloat16

NZ = 16
NP = 16
V = 16
K = 16
T = 32
D = 1024
DIRECT = 2
TILES = 9
FAR_FIRST = (8, 7, 9, 6, 10, 5, 11, 4, 12, 3, 13, 2, 14, 1, 15)
PLANE_STEPS = sorted(
    [(dx, dy) for dx in range(4) for dy in range(4) if dx or dy],
    key=lambda step: -sum(min(d, 4 - d) for d in step),
)
VK = V * K
TOK = NP * T


def dot(a, b, ca=1, cb=0):
    return lax.dot_general(a, b, (((ca,), (cb,)), ((), ())), preferred_element_type=F32)


def pooling_kernel(
    owner_hbm,
    band_hbm,
    fields_hbm,
    pw_hbm,
    ve_hbm,
    kq_hbm,
    vw_hbm,
    ow_hbm,
    cot_hbm,
    agg_ref,
    dvw_ref,
    dpw_ref,
    owner_ref,
    band_ref,
    fields_v,
    pwve,
    kq_v,
    vwg,
    vw_v,
    ow_v,
    cot_v,
    fmsg,
    recv0,
    wmsg,
    recv1,
    hmsg,
    recvh,
    mm,
    fturn,
    pturn,
    recvf,
    recvp,
    aa,
    pmsg,
    recvpool,
    gtile,
    recvr,
    recvb,
    quad,
    quadb,
    recvq,
    recvx,
    recvqb,
    gtot,
    msg5,
    recv5,
    load_sem,
    send_sem,
    recv_sem,
):
    z = lax.axis_index("var")
    lat = lax.axis_index("lat")
    core = lax.rem(lat, 2)
    p = lat // 2

    x, y = p // 4, lax.rem(p, 4)
    sibling = {"var": z, "lat": p * 2 + 1 - core}

    def zpeer(d):
        return {"var": lax.rem(z + d, NZ), "lat": lat}

    def other_core(zt):
        return {"var": zt, "lat": p * 2 + 1 - core}

    def plane_chip(step):
        return lax.rem(x + step[0], 4) * 4 + lax.rem(y + step[1], 4)

    def plane_peer(chip):
        return {"var": z, "lat": chip * 2 + core}

    def quad_device(j):
        return {"var": (z // 4) * 4 + lax.rem(j, 4), "lat": p * 2 + j // 4}

    barrier = pltpu.get_barrier_semaphore()

    def signal(device):
        pl.semaphore_signal(barrier, inc=1, device_id=device, device_id_type=MESH)

    own_j = core * 4 + lax.rem(z, 4)
    for d in FAR_FIRST:
        signal(zpeer(d))

    @pl.when(z < DIRECT)
    def _():
        for d in FAR_FIRST:
            signal(other_core(lax.rem(z + d, NZ)))

    @pl.when(z >= DIRECT)
    def _():
        for d in range(1, 4):
            signal(other_core((z // 4) * 4 + lax.rem(z + d, 4)))

    for step in PLANE_STEPS:
        signal(plane_peer(plane_chip(step)))
    signal(sibling)
    def whole(ref, slot):
        return pltpu.make_async_remote_copy(
            src_ref=ref,
            dst_ref=ref,
            send_sem=send_sem.at[slot],
            recv_sem=recv_sem.at[slot],
            device_id=sibling,
            device_id_type=MESH,
        )

    def send(src, dst, slot, device):
        pltpu.make_async_remote_copy(
            src_ref=src,
            dst_ref=dst,
            send_sem=send_sem.at[slot],
            recv_sem=recv_sem.at[slot],
            device_id=device,
            device_id_type=MESH,
        ).start()

    def send_plane(src, dst, slot):
        for step in PLANE_STEPS:
            chip = plane_chip(step)
            send(src(chip), dst, slot, plane_peer(chip))

    group = pl.multiple_of((p // 2) * 128, 128)
    loads = [
        pltpu.make_async_copy(fields_hbm, fields_v, load_sem.at[4]),
        pltpu.make_async_copy(pw_hbm, pwve.at[pl.ds(0, 32)], load_sem.at[0]),
        pltpu.make_async_copy(ve_hbm, pwve.at[pl.ds(32, 16)], load_sem.at[1]),
        pltpu.make_async_copy(vw_hbm.at[:, pl.ds(group, 128)], vwg, load_sem.at[2]),
        pltpu.make_async_copy(kq_hbm, kq_v, load_sem.at[3]),
        pltpu.make_async_copy(cot_hbm, cot_v, load_sem.at[5]),
        pltpu.make_async_copy(ow_hbm, ow_v, load_sem.at[6]),
        pltpu.make_async_copy(vw_hbm, vw_v, load_sem.at[7]),
        pltpu.make_async_copy(owner_hbm, owner_ref, load_sem.at[8]),
        pltpu.make_async_copy(band_hbm, band_ref, load_sem.at[9]),
    ]
    for load in loads[8:] + loads[:8]:
        load.start()

    lane16 = lax.broadcasted_iota(jnp.int32, (16, 128), 1)
    row16 = lax.broadcasted_iota(jnp.int32, (16, 128), 0)
    lane32 = lax.broadcasted_iota(jnp.int32, (32, 128), 1)
    loads[0].wait()
    for q in range(4):
        low = fields_v[0, :, 128 * q : 128 * q + 128].astype(F32)
        high = fields_v[1, :, 128 * q : 128 * q + 128].astype(F32)
        for r in range(4):
            left = pltpu.roll(low, (128 - 32 * r) % 128, 1) if r else low
            right = pltpu.roll(high, (160 - 32 * r) % 128, 1) if r != 1 else high
            piece = jnp.where(lane16 < 32, left, jnp.where(lane16 < 64, right, 0.0))
            fmsg[4 * q + r] = piece.astype(BF16)

    loads[8].wait()
    owners = [owner_ref[v] for v in range(V)]
    slots = []
    for v in range(V):
        rank = jnp.int32(0)
        for u in range(v):
            rank = rank + (owners[u] == owners[v]).astype(jnp.int32)
        slots.append(owners[v] * 2 + rank)
    held = []
    for s in range(2):
        var_of, has = jnp.int32(0), jnp.int32(0)
        for v in range(V):
            hit = (slots[v] == 2 * z + s).astype(jnp.int32)
            var_of, has = var_of + hit * v, has + hit
        held.append((var_of, has))

    for i in range(1, 5):
        loads[i].wait()
    turn = lax.rem(p, 2) * 64
    both = pwve[...]
    head_cols = pltpu.roll(dot(both, vwg[...]), turn, 1)
    key_cols = dot(both, kq_v[...], 1, 1)
    key_lane = lax.broadcasted_iota(jnp.int32, (48, 16), 1)
    key_col = jnp.sum(jnp.where(key_lane == p, key_cols, 0.0), axis=1, keepdims=True)
    key_bias = key_col[32:48]
    mm[V] = jnp.where(lane16 < 64, head_cols[32:48], 0.0).astype(BF16)
    own_group = pl.multiple_of((lat // 4) * 128, 128)
    own_cols = pltpu.roll(
        pwve[pl.ds(0, 32), pl.ds(own_group, 128)].astype(F32),
        lax.rem(192 - 32 * lax.rem(lat, 4), 128),
        1,
    )
    key_top = key_col[0:32].astype(BF16).astype(F32)
    key_mid = (key_col[0:32] - key_top).astype(BF16).astype(F32)
    key_low = key_col[0:32] - key_top - key_mid
    packed = jnp.where(lane32 < 64, head_cols[0:32], own_cols)
    packed = jnp.where(lane32 < 96, packed, jnp.where(lane32 == 96, key_top, 0.0))
    packed = jnp.where(lane32 == 97, key_mid, jnp.where(lane32 == 98, key_low, packed))
    wmsg[...] = packed.astype(BF16).reshape(2, 16, 128)

    pl.semaphore_wait(barrier, jnp.where(z < 4, 34, 34 + DIRECT))

    for d in FAR_FIRST:
        send(fmsg.at[lax.rem(z + d, NZ)], recv0.at[z], 0, zpeer(d))
    for d in FAR_FIRST:
        send(wmsg, recv1.at[pl.ds(2 * z, 2)], 1, zpeer(d))
    recv0[z] = fmsg[z]
    recv1[pl.ds(2 * z, 2)] = wmsg[...]

    loads[5].wait()
    loads[9].wait()
    count = band_ref[lat]
    rows = z * T + lax.broadcasted_iota(jnp.int32, (T, 1), 0)
    valid = (rows < count).astype(F32)
    masked = (cot_v[...].astype(F32) * valid).astype(BF16)
    loads[6].wait()
    head_grads = dot(masked, ow_v[...], 1, 1)
    for q in range(8):
        two = head_grads[:, 128 * q : 128 * q + 128]
        turned = pltpu.roll(two, 64, 1)
        hmsg[2 * q] = jnp.where(lane16 < 64, two[0:16], turned[16:32]).astype(BF16)
        hmsg[2 * q + 1] = jnp.where(lane16 < 64, turned[0:16], two[16:32]).astype(BF16)

    send_plane(lambda chip: hmsg.at[chip], recvh.at[p], 2)
    recvh[p] = hmsg[p]

    whole(recv0.at[pl.ds(0, 15)], 0).wait_recv()
    pieces = []
    for v in range(V):
        tile = recv0[slots[v] // 2].astype(F32)
        pieces.append(pltpu.roll(tile, lax.rem(128 - 32 * lax.rem(slots[v], 2), 128), 1))
    fturn[...] = jnp.concatenate(pieces, axis=0).T[0:32].astype(BF16)
    send_plane(lambda chip: fturn, recvf.at[p], 3)
    recvf[p] = fturn[...]

    whole(recv1.at[pl.ds(0, 30)], 1).wait_recv()
    for v in range(V):
        mm[v] = recv1[slots[v]]
    chosen = mm[pl.ds(0, V)].reshape(VK, 128).astype(F32)
    lane_all = lax.broadcasted_iota(jnp.int32, (VK, 128), 1)
    key_rows = jnp.sum(
        jnp.where((lane_all >= 96) & (lane_all < 99), chosen, 0.0), axis=1, keepdims=True
    ).reshape(V, K, 1)
    pturn[...] = chosen.T[64:96].astype(BF16)
    send_plane(lambda chip: pturn, recvp.at[p], 4)
    recvp[p] = pturn[...]

    whole(recvh.at[pl.ds(0, 15)], 2).wait_recv()
    packed = recvh[...].astype(F32)
    unpacked = jnp.concatenate([packed, pltpu.roll(packed, 64, 2)], axis=1)
    grads = jnp.where(lane32 < 64, unpacked, 0.0).astype(BF16).reshape(TOK, 128)
    whole(recvf.at[pl.ds(0, 15)], 3).wait_recv()
    pixels = recvf[...].reshape(TOK, VK).astype(F32).T.reshape(V, K, TOK)
    scores = jnp.sum(pixels * key_rows, axis=1) + key_bias
    exponent = jnp.exp(scores)
    attention = exponent / jnp.sum(exponent, axis=0, keepdims=True)
    weighted = pixels * attention[:, None, :]
    aa[pl.ds(0, VK)] = weighted.reshape(VK, TOK).astype(BF16)
    aa[pl.ds(VK, V)] = attention.astype(BF16)
    head_weights = mm[...].reshape(VK + V, 128)
    lhs = aa[...]
    sums = dot(lhs, grads)
    cross = dot(head_weights, grads, 1, 1)
    dweights = jnp.sum(pixels * cross[0:VK].reshape(V, K, TOK), axis=1) + cross[VK : VK + V]
    dscores = attention * (
        dweights - jnp.sum(attention * dweights, axis=0, keepdims=True)
    )
    score_sums = jnp.sum(pixels * dscores[:, None, :], axis=2, keepdims=True)
    score_rows = jnp.sum(jnp.where(lane16 == 64 + row16, score_sums, 0.0), axis=1)
    dense = sums[0:128] + pltpu.roll(sums[128:256], 64, 1)
    gtile[pl.ds(0, 8)] = dense.astype(BF16).reshape(8, 16, 128)
    gtile[8] = (sums[VK : VK + V] + score_rows).astype(BF16)

    for d in range(1, 8):
        j = lax.rem(own_j + d, 8)
        send(gtile.at[j], recvr.at[own_j], 5, quad_device(j))
    recvr[own_j] = gtile[own_j]
    has_bias = own_j == 1

    @pl.when(has_bias)
    def _():
        recvb[own_j] = gtile[8]

    @pl.when(jnp.logical_not(has_bias))
    def _():
        send(gtile.at[8], recvb.at[own_j], 6, quad_device(jnp.int32(1)))

    pooled = dot(lhs, head_weights, 0, 0)
    pmsg[...] = pooled.astype(BF16).reshape(NP, T, 128)

    whole(recvr.at[pl.ds(0, 7)], 5).wait_recv()
    quad[...] = jnp.sum(recvr[...].astype(F32), axis=0).astype(BF16)
    for zt in range(DIRECT):
        send(quad, recvx.at[z], 14, other_core(zt))
    for d in FAR_FIRST:
        send(quad, recvq.at[z], 10, zpeer(d))
    recvq[z] = quad[...]

    @pl.when(has_bias)
    def _():
        whole(recvb.at[pl.ds(0, 7)], 6).wait_recv()
        quadb[...] = jnp.sum(recvb[...].astype(F32), axis=0).astype(BF16)
        for zt in range(DIRECT):
            send(quadb, recvqb.at[z // 4], 11, other_core(zt))
        for d in FAR_FIRST:
            send(quadb, recvqb.at[z // 4], 11, zpeer(d))
        recvqb[z // 4] = quadb[...]

    send_plane(lambda chip: pmsg.at[chip], recvpool.at[p], 7)
    recvpool[p] = pmsg[p]

    whole(recvp.at[pl.ds(0, 15)], 4).wait_recv()
    whole(recvpool.at[pl.ds(0, 15)], 7).wait_recv()
    parts = []
    for q in range(8):
        left = recvpool[2 * q].astype(F32)
        right = recvpool[2 * q + 1].astype(F32)
        parts.append(jnp.where(lane32 < 64, left, pltpu.roll(right, 64, 1)).astype(BF16))
    projected = dot(jnp.concatenate(parts, axis=1), ow_v[...])
    agg_ref[...] = (projected * valid).astype(BF16)

    whole(recvq.at[pl.ds(0, 15)], 10).wait_recv()
    half_at = pl.multiple_of(5 * core, 5)
    rest_at = pl.multiple_of(5 - 5 * core, 5)
    direct = z < DIRECT

    def four_tiles(ref):
        return jnp.sum(ref[...].astype(F32).reshape(4, 4, 16, 128), axis=0).astype(BF16)

    gtot[pl.ds(half_at, 4)] = four_tiles(recvq)

    @pl.when((core == 0) & has_bias)
    def _():
        whole(recvqb.at[pl.ds(0, 3)], 11).wait_recv()

    @pl.when(((core == 0) & jnp.logical_not(has_bias)) | ((core == 1) & direct))
    def _():
        whole(recvqb, 11).wait_recv()

    @pl.when((core == 0) | direct)
    def _():
        gtot[4] = jnp.sum(recvqb[...].astype(F32), axis=0).astype(BF16)

    @pl.when((core == 1) & jnp.logical_not(direct))
    def _():
        gtot[9] = jnp.zeros((16, 128), BF16)

    @pl.when(direct)
    def _():
        whole(recvx, 14).wait_recv()
        gtot[pl.ds(rest_at, 4)] = four_tiles(recvx)

    @pl.when(jnp.logical_not(direct))
    def _():
        send(gtot.at[pl.ds(half_at, 5)], gtot.at[pl.ds(half_at, 5)], 12, sibling)
        whole(gtot.at[pl.ds(0, 5)], 12).wait_recv()

    bias_rows = pwve[pl.ds(32, 16)]
    rows_all = recvp[...].reshape(TOK, VK)
    patch_sums = jnp.concatenate([gtot[pl.ds(0, 4)], gtot[pl.ds(5, 4)]], axis=0).reshape(128, 128)
    bias_sums = gtot[4]
    low = dot(rows_all[:, 0:128], patch_sums)
    high = dot(rows_all[:, 128:256], patch_sums)
    bias_all = dot(bias_rows, bias_sums, 0, 0).reshape(NP, 2, T, 128)
    bias = jnp.where(core == 0, bias_all[:, 0], bias_all[:, 1])
    value_rows = (low + pltpu.roll(high, 64, 1)).reshape(NP, T, 128) + bias
    picked, score_parts = [], []
    for s in range(2):
        var_of, has = held[s]
        at = lax.rem(var_of, 8)
        tile = gtot[at + at // 4].astype(F32)
        tile = jnp.where(var_of < 8, pltpu.roll(tile, 64, 1), tile)
        picked.append(tile * has.astype(F32))
        line = jnp.where((row16 == var_of) & (lane16 >= 64) & (lane16 < 80), bias_sums.astype(F32), 0.0)
        line = jnp.sum(line, axis=0, keepdims=True) * has.astype(F32)
        score_parts.append(pltpu.roll(line, 64 + 16 * s, 1))
    mine = jnp.concatenate(picked, axis=0)
    score_line = jnp.broadcast_to(score_parts[0] + score_parts[1], (16, 128)).astype(BF16)
    msg5[:, 0:32, :] = jnp.where(lane32 < 64, value_rows, mine).astype(BF16)
    msg5[:, 32:48, :] = jnp.broadcast_to(score_line, (NP, 16, 128))
    for step in PLANE_STEPS:
        chip = plane_chip(step)
        slot = {0: 8, 1: 9, 3: 9, 2: 13}[step[0]]
        send(msg5.at[chip], recv5.at[p], slot, plane_peer(chip))
    recv5[p] = msg5[p]

    loads[7].wait()
    patch_grad = jnp.zeros((32, D), F32)
    score_lines = jnp.zeros((16, 128), F32)
    for i, dx in enumerate((0, 1, 3, 2)):
        if i == 0:
            whole(recv5.at[pl.ds(0, 3)], 8).wait_recv()
        if i == 1:
            whole(recv5.at[pl.ds(0, 8)], 9).wait_recv()
        if i == 3:
            whole(recv5.at[pl.ds(0, 4)], 13).wait_recv()
        row = lax.rem(x + dx, 4)
        parts = []
        for q in range(2):
            left = recv5[4 * row + 2 * q, 0:32].astype(F32)
            right = recv5[4 * row + 2 * q + 1, 0:32].astype(F32)
            at = pl.multiple_of(256 * row + 128 * q, 128)
            dvw_ref[:, pl.ds(at, 128)] = jnp.where(lane32 < 64, left, pltpu.roll(right, 64, 1))
            parts.append(jnp.where(lane32 < 64, pltpu.roll(left, 64, 1), right).astype(BF16))
        columns = vw_v[:, pl.ds(pl.multiple_of(256 * row, 256), 256)]
        patch_grad = patch_grad + dot(jnp.concatenate(parts, axis=1), columns, 1, 1)
        for q in range(4):
            line = recv5[4 * row + q, 32:48].astype(F32)
            score_lines = jnp.where(row16 == 4 * row + q, line, score_lines)
    score_grad = score_lines.T[0:32].astype(BF16)
    dpw_ref[...] = patch_grad + dot(score_grad, kq_v[...])

    whole(recv0.at[pl.ds(0, 15)], 0).wait_send()
    whole(recv1.at[pl.ds(0, 30)], 1).wait_send()
    whole(recvh.at[pl.ds(0, 15)], 2).wait_send()
    whole(recvf.at[pl.ds(0, 15)], 3).wait_send()
    whole(recvp.at[pl.ds(0, 15)], 4).wait_send()
    whole(recvr.at[pl.ds(0, 7)], 5).wait_send()
    whole(recvpool.at[pl.ds(0, 15)], 7).wait_send()
    whole(recv5.at[pl.ds(0, 3)], 8).wait_send()
    whole(recv5.at[pl.ds(0, 8)], 9).wait_send()
    whole(recv5.at[pl.ds(0, 4)], 13).wait_send()
    whole(recvq.at[pl.ds(0, 15)], 10).wait_send()
    whole(recvx.at[pl.ds(0, DIRECT)], 14).wait_send()

    @pl.when(jnp.logical_not(direct))
    def _():
        whole(gtot.at[pl.ds(0, 5)], 12).wait_send()


    @pl.when(has_bias)
    def _():
        whole(recv1.at[pl.ds(0, 15 + DIRECT)], 11).wait_send()

    @pl.when(jnp.logical_not(has_bias))
    def _():
        whole(quadb, 6).wait_send()


def place_kernel(*refs):
    sources, results, sems = refs[:3], refs[3:6], refs[6]
    stores = [pltpu.make_async_copy(sources[i], results[i], sems.at[i]) for i in range(3)]
    for store in stores:
        store.start()
    for store in stores:
        store.wait()


def per_device(
    fields,
    owner_table,
    band_tokens,
    patch_weight,
    var_embed,
    key_query,
    value_weight,
    out_weight,
    cotangent,
):
    hbm_spec = pl.BlockSpec(memory_space=pltpu.HBM)
    vmem_spec = pl.BlockSpec(memory_space=pltpu.VMEM)
    aggregated, value_grad, patch_grad = pl.pallas_call(
        pooling_kernel,
        out_shape=(
            pltpu.VMEM((T, D), BF16),
            pltpu.VMEM((32, D), F32),
            pltpu.VMEM((32, D), F32),
        ),
        in_specs=[hbm_spec] * 9,
        out_specs=(vmem_spec, vmem_spec, vmem_spec),
        scratch_shapes=[
            pltpu.SMEM((V,), jnp.int32),
            pltpu.SMEM((2 * NP,), jnp.int32),
            pltpu.VMEM((2, K, 512), BF16),
            pltpu.VMEM((48, D), BF16),
            pltpu.VMEM((16, D), BF16),
            pltpu.VMEM((D, 128), BF16),
            pltpu.VMEM((D, D), BF16),
            pltpu.VMEM((D, D), BF16),
            pltpu.VMEM((T, D), BF16),
            pltpu.VMEM((NZ, K, 128), BF16),
            pltpu.VMEM((NZ, K, 128), BF16),
            pltpu.VMEM((2, K, 128), BF16),
            pltpu.VMEM((2 * NZ, K, 128), BF16),
            pltpu.VMEM((NP, 16, 128), BF16),
            pltpu.VMEM((NP, 16, 128), BF16),
            pltpu.VMEM((V + 1, K, 128), BF16),
            pltpu.VMEM((T, VK), BF16),
            pltpu.VMEM((32, VK), BF16),
            pltpu.VMEM((NP, T, VK), BF16),
            pltpu.VMEM((NP, T, VK), BF16),
            pltpu.VMEM((VK + V, TOK), BF16),
            pltpu.VMEM((NP, T, 128), BF16),
            pltpu.VMEM((NP, T, 128), BF16),
            pltpu.VMEM((TILES, 16, 128), BF16),
            pltpu.VMEM((8, 16, 128), BF16),
            pltpu.VMEM((8, 16, 128), BF16),
            pltpu.VMEM((16, 128), BF16),
            pltpu.VMEM((16, 128), BF16),
            pltpu.VMEM((NZ, 16, 128), BF16),
            pltpu.VMEM((NZ, 16, 128), BF16),
            pltpu.VMEM((4, 16, 128), BF16),
            pltpu.VMEM((10, 16, 128), BF16),
            pltpu.VMEM((NP, 48, 128), BF16),
            pltpu.VMEM((NP, 48, 128), BF16),
            pltpu.SemaphoreType.DMA((10,)),
            pltpu.SemaphoreType.DMA((15,)),
            pltpu.SemaphoreType.DMA((15,)),
        ],
        compiler_params=pltpu.CompilerParams(
            collective_id=0, has_side_effects=True, vmem_limit_bytes=60 * 1024 * 1024
        ),
        cost_estimate=pl.CostEstimate(
            flops=2_000_000_000, bytes_accessed=5_000_000, transcendentals=8192
        ),
    )(
        owner_table,
        band_tokens,
        fields,
        patch_weight.reshape(32, D),
        var_embed,
        key_query.T,
        value_weight,
        out_weight,
        cotangent.reshape(T, D),
    )
    aggregated, value_grad, patch_grad = pl.pallas_call(
        place_kernel,
        out_shape=(
            jax.ShapeDtypeStruct((T, D), BF16),
            jax.ShapeDtypeStruct((32, D), F32),
            jax.ShapeDtypeStruct((32, D), F32),
        ),
        in_specs=[hbm_spec] * 3,
        out_specs=(hbm_spec,) * 3,
        scratch_shapes=[pltpu.SemaphoreType.DMA((3,))],
        compiler_params=pltpu.CompilerParams(vmem_limit_bytes=4 * 1024 * 1024),
    )(aggregated, value_grad, patch_grad)
    return (
        aggregated.reshape(1, T, D),
        value_grad,
        patch_grad.reshape(2, K, D),
    )


def solution(mesh):
    in_specs = (
        P("var", None, "lat"),
        P(),
        P(),
        P("var", None, None),
        P(),
        P(),
        P(),
        P(),
        P("lat", "var", None),
    )
    out_specs = (P("lat", "var", None), P("lat", None), P("var", None, None))
    return jax.shard_map(
        per_device, mesh=mesh, in_specs=in_specs, out_specs=out_specs, check_vma=False
    )
```

```python
import functools

import jax
import jax.numpy as jnp
from jax import lax
from jax.experimental import pallas as pl
from jax.experimental.pallas import tpu as pltpu
from jax.sharding import PartitionSpec as P

MESH = pl.DeviceIdType.MESH
F32 = jnp.float32
BF16 = jnp.bfloat16

NZ = 16
NP = 16
V = 16
K = 16
T = 32
D = 1024
DIRECT = 2
TILES = 9
FAR_FIRST = (8, 7, 9, 6, 10, 5, 11, 4, 12, 3, 13, 2, 14, 1, 15)
PLANE_STEPS = sorted(
    [(dx, dy) for dx in range(4) for dy in range(4) if dx or dy],
    key=lambda step: -sum(min(d, 4 - d) for d in step),
)
VK = V * K
TOK = NP * T


def dot(a, b, ca=1, cb=0):
    return lax.dot_general(a, b, (((ca,), (cb,)), ((), ())), preferred_element_type=F32)


def pooling_kernel(
    owner_hbm,
    band_hbm,
    fields_hbm,
    pw_hbm,
    ve_hbm,
    kq_hbm,
    vw_hbm,
    ow_hbm,
    cot_hbm,
    agg_ref,
    dvw_ref,
    dpw_ref,
    owner_ref,
    band_ref,
    fields_v,
    pwve,
    kq_v,
    vwg,
    vw_v,
    ow_v,
    cot_v,
    fmsg,
    recv0,
    wmsg,
    recv1,
    hmsg,
    recvh,
    mm,
    fturn,
    pturn,
    recvf,
    recvp,
    aa,
    pmsg,
    recvpool,
    gtile,
    recvr,
    recvb,
    quad,
    quadb,
    recvq,
    recvx,
    recvqb,
    gtot,
    msg5,
    recv5,
    load_sem,
    send_sem,
    recv_sem,
):
    z = lax.axis_index("var")
    lat = lax.axis_index("lat")
    core = lax.rem(lat, 2)
    p = lat // 2

    x, y = p // 4, lax.rem(p, 4)
    sibling = {"var": z, "lat": p * 2 + 1 - core}

    def zpeer(d):
        return {"var": lax.rem(z + d, NZ), "lat": lat}

    def other_core(zt):
        return {"var": zt, "lat": p * 2 + 1 - core}

    def plane_chip(step):
        return lax.rem(x + step[0], 4) * 4 + lax.rem(y + step[1], 4)

    def plane_peer(chip):
        return {"var": z, "lat": chip * 2 + core}

    def quad_device(j):
        return {"var": (z // 4) * 4 + lax.rem(j, 4), "lat": p * 2 + j // 4}

    barrier = pltpu.get_barrier_semaphore()

    def signal(device):
        pl.semaphore_signal(barrier, inc=1, device_id=device, device_id_type=MESH)

    own_j = core * 4 + lax.rem(z, 4)
    for d in FAR_FIRST:
        signal(zpeer(d))

    @pl.when(z < DIRECT)
    def _():
        for d in FAR_FIRST:
            signal(other_core(lax.rem(z + d, NZ)))

    @pl.when(z >= DIRECT)
    def _():
        for d in range(1, 4):
            signal(other_core((z // 4) * 4 + lax.rem(z + d, 4)))

    for step in PLANE_STEPS:
        signal(plane_peer(plane_chip(step)))
    signal(sibling)
    def whole(ref, slot):
        return pltpu.make_async_remote_copy(
            src_ref=ref,
            dst_ref=ref,
            send_sem=send_sem.at[slot],
            recv_sem=recv_sem.at[slot],
            device_id=sibling,
            device_id_type=MESH,
        )

    def send(src, dst, slot, device):
        pltpu.make_async_remote_copy(
            src_ref=src,
            dst_ref=dst,
            send_sem=send_sem.at[slot],
            recv_sem=recv_sem.at[slot],
            device_id=device,
            device_id_type=MESH,
        ).start()

    def send_plane(src, dst, slot):
        for step in PLANE_STEPS:
            chip = plane_chip(step)
            send(src(chip), dst, slot, plane_peer(chip))

    group = pl.multiple_of((p // 2) * 128, 128)
    loads = [
        pltpu.make_async_copy(fields_hbm, fields_v, load_sem.at[4]),
        pltpu.make_async_copy(pw_hbm, pwve.at[pl.ds(0, 32)], load_sem.at[0]),
        pltpu.make_async_copy(ve_hbm, pwve.at[pl.ds(32, 16)], load_sem.at[1]),
        pltpu.make_async_copy(vw_hbm.at[:, pl.ds(group, 128)], vwg, load_sem.at[2]),
        pltpu.make_async_copy(kq_hbm, kq_v, load_sem.at[3]),
        pltpu.make_async_copy(cot_hbm, cot_v, load_sem.at[5]),
        pltpu.make_async_copy(ow_hbm, ow_v, load_sem.at[6]),
        pltpu.make_async_copy(vw_hbm, vw_v, load_sem.at[7]),
        pltpu.make_async_copy(owner_hbm, owner_ref, load_sem.at[8]),
        pltpu.make_async_copy(band_hbm, band_ref, load_sem.at[9]),
    ]
    for load in loads[8:] + loads[:8]:
        load.start()

    lane16 = lax.broadcasted_iota(jnp.int32, (16, 128), 1)
    row16 = lax.broadcasted_iota(jnp.int32, (16, 128), 0)
    lane32 = lax.broadcasted_iota(jnp.int32, (32, 128), 1)
    loads[0].wait()
    for q in range(4):
        low = fields_v[0, :, 128 * q : 128 * q + 128].astype(F32)
        high = fields_v[1, :, 128 * q : 128 * q + 128].astype(F32)
        for r in range(4):
            left = pltpu.roll(low, (128 - 32 * r) % 128, 1) if r else low
            right = pltpu.roll(high, (160 - 32 * r) % 128, 1) if r != 1 else high
            piece = jnp.where(lane16 < 32, left, jnp.where(lane16 < 64, right, 0.0))
            fmsg[4 * q + r] = piece.astype(BF16)

    loads[8].wait()
    owners = [owner_ref[v] for v in range(V)]
    slots = []
    for v in range(V):
        rank = jnp.int32(0)
        for u in range(v):
            rank = rank + (owners[u] == owners[v]).astype(jnp.int32)
        slots.append(owners[v] * 2 + rank)
    held = []
    for s in range(2):
        var_of, has = jnp.int32(0), jnp.int32(0)
        for v in range(V):
            hit = (slots[v] == 2 * z + s).astype(jnp.int32)
            var_of, has = var_of + hit * v, has + hit
        held.append((var_of, has))

    for i in range(1, 5):
        loads[i].wait()
    turn = lax.rem(p, 2) * 64
    both = pwve[...]
    head_cols = pltpu.roll(dot(both, vwg[...]), turn, 1)
    key_cols = dot(both, kq_v[...], 1, 1)
    key_lane = lax.broadcasted_iota(jnp.int32, (48, 16), 1)
    key_col = jnp.sum(jnp.where(key_lane == p, key_cols, 0.0), axis=1, keepdims=True)
    key_bias = key_col[32:48]
    mm[V] = jnp.where(lane16 < 64, head_cols[32:48], 0.0).astype(BF16)
    own_group = pl.multiple_of((lat // 4) * 128, 128)
    own_cols = pltpu.roll(
        pwve[pl.ds(0, 32), pl.ds(own_group, 128)].astype(F32),
        lax.rem(192 - 32 * lax.rem(lat, 4), 128),
        1,
    )
    key_top = key_col[0:32].astype(BF16).astype(F32)
    key_mid = (key_col[0:32] - key_top).astype(BF16).astype(F32)
    key_low = key_col[0:32] - key_top - key_mid
    packed = jnp.where(lane32 < 64, head_cols[0:32], own_cols)
    packed = jnp.where(lane32 < 96, packed, jnp.where(lane32 == 96, key_top, 0.0))
    packed = jnp.where(lane32 == 97, key_mid, jnp.where(lane32 == 98, key_low, packed))
    wmsg[...] = packed.astype(BF16).reshape(2, 16, 128)

    pl.semaphore_wait(barrier, jnp.where(z < 4, 34, 34 + DIRECT))

    for d in FAR_FIRST:
        send(fmsg.at[lax.rem(z + d, NZ)], recv0.at[z], 0, zpeer(d))
    for d in FAR_FIRST:
        send(wmsg, recv1.at[pl.ds(2 * z, 2)], 1, zpeer(d))
    recv0[z] = fmsg[z]
    recv1[pl.ds(2 * z, 2)] = wmsg[...]

    loads[5].wait()
    loads[9].wait()
    count = band_ref[lat]
    rows = z * T + lax.broadcasted_iota(jnp.int32, (T, 1), 0)
    valid = (rows < count).astype(F32)
    masked = (cot_v[...].astype(F32) * valid).astype(BF16)
    loads[6].wait()
    head_grads = dot(masked, ow_v[...], 1, 1)
    for q in range(8):
        two = head_grads[:, 128 * q : 128 * q + 128]
        turned = pltpu.roll(two, 64, 1)
        hmsg[2 * q] = jnp.where(lane16 < 64, two[0:16], turned[16:32]).astype(BF16)
        hmsg[2 * q + 1] = jnp.where(lane16 < 64, turned[0:16], two[16:32]).astype(BF16)

    send_plane(lambda chip: hmsg.at[chip], recvh.at[p], 2)
    recvh[p] = hmsg[p]

    whole(recv0.at[pl.ds(0, 15)], 0).wait_recv()
    pieces = []
    for v in range(V):
        tile = recv0[slots[v] // 2].astype(F32)
        pieces.append(pltpu.roll(tile, lax.rem(128 - 32 * lax.rem(slots[v], 2), 128), 1))
    fturn[...] = jnp.concatenate(pieces, axis=0).T[0:32].astype(BF16)
    send_plane(lambda chip: fturn, recvf.at[p], 3)
    recvf[p] = fturn[...]

    whole(recv1.at[pl.ds(0, 30)], 1).wait_recv()
    for v in range(V):
        mm[v] = recv1[slots[v]]
    chosen = mm[pl.ds(0, V)].reshape(VK, 128).astype(F32)
    lane_all = lax.broadcasted_iota(jnp.int32, (VK, 128), 1)
    key_rows = jnp.sum(
        jnp.where((lane_all >= 96) & (lane_all < 99), chosen, 0.0), axis=1, keepdims=True
    ).reshape(V, K, 1)
    pturn[...] = chosen.T[64:96].astype(BF16)
    send_plane(lambda chip: pturn, recvp.at[p], 4)
    recvp[p] = pturn[...]

    whole(recvh.at[pl.ds(0, 15)], 2).wait_recv()
    packed = recvh[...].astype(F32)
    unpacked = jnp.concatenate([packed, pltpu.roll(packed, 64, 2)], axis=1)
    grads = jnp.where(lane32 < 64, unpacked, 0.0).astype(BF16).reshape(TOK, 128)
    whole(recvf.at[pl.ds(0, 15)], 3).wait_recv()
    pixels = recvf[...].reshape(TOK, VK).astype(F32).T.reshape(V, K, TOK)
    scores = jnp.sum(pixels * key_rows, axis=1) + key_bias
    exponent = jnp.exp(scores)
    attention = exponent / jnp.sum(exponent, axis=0, keepdims=True)
    weighted = pixels * attention[:, None, :]
    aa[pl.ds(0, VK)] = weighted.reshape(VK, TOK).astype(BF16)
    aa[pl.ds(VK, V)] = attention.astype(BF16)
    head_weights = mm[...].reshape(VK + V, 128)
    lhs = aa[...]
    sums = dot(lhs, grads)
    cross = dot(head_weights, grads, 1, 1)
    dweights = jnp.sum(pixels * cross[0:VK].reshape(V, K, TOK), axis=1) + cross[VK : VK + V]
    dscores = attention * (
        dweights - jnp.sum(attention * dweights, axis=0, keepdims=True)
    )
    score_sums = jnp.sum(pixels * dscores[:, None, :], axis=2, keepdims=True)
    score_rows = jnp.sum(jnp.where(lane16 == 64 + row16, score_sums, 0.0), axis=1)
    dense = sums[0:128] + pltpu.roll(sums[128:256], 64, 1)
    gtile[pl.ds(0, 8)] = dense.astype(BF16).reshape(8, 16, 128)
    gtile[8] = (sums[VK : VK + V] + score_rows).astype(BF16)

    for d in range(1, 8):
        j = lax.rem(own_j + d, 8)
        send(gtile.at[j], recvr.at[own_j], 5, quad_device(j))
    recvr[own_j] = gtile[own_j]
    has_bias = own_j == 1

    @pl.when(has_bias)
    def _():
        recvb[own_j] = gtile[8]

    @pl.when(jnp.logical_not(has_bias))
    def _():
        send(gtile.at[8], recvb.at[own_j], 6, quad_device(jnp.int32(1)))

    pooled = dot(lhs, head_weights, 0, 0).reshape(NP, T, 128)
    beside = pltpu.roll(pooled[:, 16:32], 64, 2)
    pmsg[...] = jnp.where(lane16 < 64, pooled[:, 0:16], beside).astype(BF16)

    whole(recvr.at[pl.ds(0, 7)], 5).wait_recv()
    quad[...] = jnp.sum(recvr[...].astype(F32), axis=0).astype(BF16)
    for zt in range(DIRECT):
        send(quad, recvx.at[z], 14, other_core(zt))
    for d in FAR_FIRST:
        send(quad, recvq.at[z], 10, zpeer(d))
    recvq[z] = quad[...]

    @pl.when(has_bias)
    def _():
        whole(recvb.at[pl.ds(0, 7)], 6).wait_recv()
        quadb[...] = jnp.sum(recvb[...].astype(F32), axis=0).astype(BF16)
        for zt in range(DIRECT):
            send(quadb, recvqb.at[z // 4], 11, other_core(zt))
        for d in FAR_FIRST:
            send(quadb, recvqb.at[z // 4], 11, zpeer(d))
        recvqb[z // 4] = quadb[...]

    send_plane(lambda chip: pmsg.at[chip], recvpool.at[p], 7)
    recvpool[p] = pmsg[p]

    whole(recvp.at[pl.ds(0, 15)], 4).wait_recv()
    whole(recvpool.at[pl.ds(0, 15)], 7).wait_recv()
    parts = []
    for q in range(8):
        left = recvpool[2 * q].astype(F32)
        right = recvpool[2 * q + 1].astype(F32)
        upper = jnp.where(lane16 < 64, left, pltpu.roll(right, 64, 1))
        lower = jnp.where(lane16 < 64, pltpu.roll(left, 64, 1), right)
        parts.append(jnp.concatenate([upper, lower], axis=0).astype(BF16))
    projected = dot(jnp.concatenate(parts, axis=1), ow_v[...])
    agg_ref[...] = (projected * valid).astype(BF16)

    whole(recvq.at[pl.ds(0, 15)], 10).wait_recv()
    half_at = pl.multiple_of(5 * core, 5)
    rest_at = pl.multiple_of(5 - 5 * core, 5)
    direct = z < DIRECT

    def four_tiles(ref):
        return jnp.sum(ref[...].astype(F32).reshape(4, 4, 16, 128), axis=0).astype(BF16)

    gtot[pl.ds(half_at, 4)] = four_tiles(recvq)

    @pl.when((core == 0) & has_bias)
    def _():
        whole(recvqb.at[pl.ds(0, 3)], 11).wait_recv()

    @pl.when(((core == 0) & jnp.logical_not(has_bias)) | ((core == 1) & direct))
    def _():
        whole(recvqb, 11).wait_recv()

    @pl.when((core == 0) | direct)
    def _():
        gtot[4] = jnp.sum(recvqb[...].astype(F32), axis=0).astype(BF16)

    @pl.when((core == 1) & jnp.logical_not(direct))
    def _():
        gtot[9] = jnp.zeros((16, 128), BF16)

    @pl.when(direct)
    def _():
        whole(recvx, 14).wait_recv()
        gtot[pl.ds(rest_at, 4)] = four_tiles(recvx)

    @pl.when(jnp.logical_not(direct))
    def _():
        send(gtot.at[pl.ds(half_at, 5)], gtot.at[pl.ds(half_at, 5)], 12, sibling)
        whole(gtot.at[pl.ds(0, 5)], 12).wait_recv()

    bias_rows = pwve[pl.ds(32, 16)]
    rows_all = recvp[...].reshape(TOK, VK)
    patch_sums = jnp.concatenate([gtot[pl.ds(0, 4)], gtot[pl.ds(5, 4)]], axis=0).reshape(128, 128)
    bias_sums = gtot[4]
    low = dot(rows_all[:, 0:128], patch_sums)
    high = dot(rows_all[:, 128:256], patch_sums)
    bias_all = dot(bias_rows, bias_sums, 0, 0).reshape(NP, 2, T, 128)
    bias = jnp.where(core == 0, bias_all[:, 0], bias_all[:, 1])
    value_rows = (low + pltpu.roll(high, 64, 1)).reshape(NP, T, 128) + bias
    picked, score_parts = [], []
    for s in range(2):
        var_of, has = held[s]
        at = lax.rem(var_of, 8)
        tile = gtot[at + at // 4].astype(F32)
        tile = jnp.where(var_of < 8, pltpu.roll(tile, 64, 1), tile)
        picked.append(tile * has.astype(F32))
        line = jnp.where((row16 == var_of) & (lane16 >= 64) & (lane16 < 80), bias_sums.astype(F32), 0.0)
        line = jnp.sum(line, axis=0, keepdims=True) * has.astype(F32)
        score_parts.append(pltpu.roll(line, 64 + 16 * s, 1))
    mine = jnp.concatenate(picked, axis=0)
    score_line = jnp.broadcast_to(score_parts[0] + score_parts[1], (16, 128)).astype(BF16)
    msg5[:, 0:32, :] = jnp.where(lane32 < 64, value_rows, mine).astype(BF16)
    msg5[:, 32:48, :] = jnp.broadcast_to(score_line, (NP, 16, 128))
    for step in PLANE_STEPS:
        chip = plane_chip(step)
        slot = {0: 8, 1: 9, 3: 9, 2: 13}[step[0]]
        send(msg5.at[chip], recv5.at[p], slot, plane_peer(chip))
    recv5[p] = msg5[p]

    loads[7].wait()
    patch_grad = jnp.zeros((32, D), F32)
    score_lines = jnp.zeros((16, 128), F32)
    for i, dx in enumerate((0, 1, 3, 2)):
        if i == 0:
            whole(recv5.at[pl.ds(0, 3)], 8).wait_recv()
        if i == 1:
            whole(recv5.at[pl.ds(0, 8)], 9).wait_recv()
        if i == 3:
            whole(recv5.at[pl.ds(0, 4)], 13).wait_recv()
        row = lax.rem(x + dx, 4)
        parts = []
        for q in range(2):
            left = recv5[4 * row + 2 * q, 0:32].astype(F32)
            right = recv5[4 * row + 2 * q + 1, 0:32].astype(F32)
            at = pl.multiple_of(256 * row + 128 * q, 128)
            dvw_ref[:, pl.ds(at, 128)] = jnp.where(lane32 < 64, left, pltpu.roll(right, 64, 1))
            parts.append(jnp.where(lane32 < 64, pltpu.roll(left, 64, 1), right).astype(BF16))
        columns = vw_v[:, pl.ds(pl.multiple_of(256 * row, 256), 256)]
        patch_grad = patch_grad + dot(jnp.concatenate(parts, axis=1), columns, 1, 1)
        for q in range(4):
            line = recv5[4 * row + q, 32:48].astype(F32)
            score_lines = jnp.where(row16 == 4 * row + q, line, score_lines)
    score_grad = score_lines.T[0:32].astype(BF16)
    dpw_ref[...] = patch_grad + dot(score_grad, kq_v[...])

    whole(recv0.at[pl.ds(0, 15)], 0).wait_send()
    whole(recv1.at[pl.ds(0, 30)], 1).wait_send()
    whole(recvh.at[pl.ds(0, 15)], 2).wait_send()
    whole(recvf.at[pl.ds(0, 15)], 3).wait_send()
    whole(recvp.at[pl.ds(0, 15)], 4).wait_send()
    whole(recvr.at[pl.ds(0, 7)], 5).wait_send()
    whole(recvpool.at[pl.ds(0, 15)], 7).wait_send()
    whole(recv5.at[pl.ds(0, 3)], 8).wait_send()
    whole(recv5.at[pl.ds(0, 8)], 9).wait_send()
    whole(recv5.at[pl.ds(0, 4)], 13).wait_send()
    whole(recvq.at[pl.ds(0, 15)], 10).wait_send()
    whole(recvx.at[pl.ds(0, DIRECT)], 14).wait_send()

    @pl.when(jnp.logical_not(direct))
    def _():
        whole(gtot.at[pl.ds(0, 5)], 12).wait_send()


    @pl.when(has_bias)
    def _():
        whole(recv1.at[pl.ds(0, 15 + DIRECT)], 11).wait_send()

    @pl.when(jnp.logical_not(has_bias))
    def _():
        whole(quadb, 6).wait_send()


def place_kernel(*refs):
    sources, results, sems = refs[:3], refs[3:6], refs[6]
    stores = [pltpu.make_async_copy(sources[i], results[i], sems.at[i]) for i in range(3)]
    for store in stores:
        store.start()
    for store in stores:
        store.wait()


def per_device(
    fields,
    owner_table,
    band_tokens,
    patch_weight,
    var_embed,
    key_query,
    value_weight,
    out_weight,
    cotangent,
):
    hbm_spec = pl.BlockSpec(memory_space=pltpu.HBM)
    vmem_spec = pl.BlockSpec(memory_space=pltpu.VMEM)
    aggregated, value_grad, patch_grad = pl.pallas_call(
        pooling_kernel,
        out_shape=(
            pltpu.VMEM((T, D), BF16),
            pltpu.VMEM((32, D), F32),
            pltpu.VMEM((32, D), F32),
        ),
        in_specs=[hbm_spec] * 9,
        out_specs=(vmem_spec, vmem_spec, vmem_spec),
        scratch_shapes=[
            pltpu.SMEM((V,), jnp.int32),
            pltpu.SMEM((2 * NP,), jnp.int32),
            pltpu.VMEM((2, K, 512), BF16),
            pltpu.VMEM((48, D), BF16),
            pltpu.VMEM((16, D), BF16),
            pltpu.VMEM((D, 128), BF16),
            pltpu.VMEM((D, D), BF16),
            pltpu.VMEM((D, D), BF16),
            pltpu.VMEM((T, D), BF16),
            pltpu.VMEM((NZ, K, 128), BF16),
            pltpu.VMEM((NZ, K, 128), BF16),
            pltpu.VMEM((2, K, 128), BF16),
            pltpu.VMEM((2 * NZ, K, 128), BF16),
            pltpu.VMEM((NP, 16, 128), BF16),
            pltpu.VMEM((NP, 16, 128), BF16),
            pltpu.VMEM((V + 1, K, 128), BF16),
            pltpu.VMEM((T, VK), BF16),
            pltpu.VMEM((32, VK), BF16),
            pltpu.VMEM((NP, T, VK), BF16),
            pltpu.VMEM((NP, T, VK), BF16),
            pltpu.VMEM((VK + V, TOK), BF16),
            pltpu.VMEM((NP, 16, 128), BF16),
            pltpu.VMEM((NP, 16, 128), BF16),
            pltpu.VMEM((TILES, 16, 128), BF16),
            pltpu.VMEM((8, 16, 128), BF16),
            pltpu.VMEM((8, 16, 128), BF16),
            pltpu.VMEM((16, 128), BF16),
            pltpu.VMEM((16, 128), BF16),
            pltpu.VMEM((NZ, 16, 128), BF16),
            pltpu.VMEM((NZ, 16, 128), BF16),
            pltpu.VMEM((4, 16, 128), BF16),
            pltpu.VMEM((10, 16, 128), BF16),
            pltpu.VMEM((NP, 48, 128), BF16),
            pltpu.VMEM((NP, 48, 128), BF16),
            pltpu.SemaphoreType.DMA((10,)),
            pltpu.SemaphoreType.DMA((15,)),
            pltpu.SemaphoreType.DMA((15,)),
        ],
        compiler_params=pltpu.CompilerParams(
            collective_id=0, has_side_effects=True, vmem_limit_bytes=60 * 1024 * 1024
        ),
        cost_estimate=pl.CostEstimate(
            flops=2_000_000_000, bytes_accessed=5_000_000, transcendentals=8192
        ),
    )(
        owner_table,
        band_tokens,
        fields,
        patch_weight.reshape(32, D),
        var_embed,
        key_query.T,
        value_weight,
        out_weight,
        cotangent.reshape(T, D),
    )
    aggregated, value_grad, patch_grad = pl.pallas_call(
        place_kernel,
        out_shape=(
            jax.ShapeDtypeStruct((T, D), BF16),
            jax.ShapeDtypeStruct((32, D), F32),
            jax.ShapeDtypeStruct((32, D), F32),
        ),
        in_specs=[hbm_spec] * 3,
        out_specs=(hbm_spec,) * 3,
        scratch_shapes=[pltpu.SemaphoreType.DMA((3,))],
        compiler_params=pltpu.CompilerParams(vmem_limit_bytes=4 * 1024 * 1024),
    )(aggregated, value_grad, patch_grad)
    return (
        aggregated.reshape(1, T, D),
        value_grad,
        patch_grad.reshape(2, K, D),
    )


def solution(mesh):
    in_specs = (
        P("var", None, "lat"),
        P(),
        P(),
        P("var", None, None),
        P(),
        P(),
        P(),
        P(),
        P("lat", "var", None),
    )
    out_specs = (P("lat", "var", None), P("lat", None), P("var", None, None))
    return jax.shard_map(
        per_device, mesh=mesh, in_specs=in_specs, out_specs=out_specs, check_vma=False
    )
```
